256 devices in a mesh: win: 4 (over y), pair: 64 (over x, z, core).
Axes of the slice: x: 4, y: 4, z: 8, core: 2. Of those that a mesh axis runs over, the one named last changes fastest.
Arguments:
- spectra: bfloat16 [512, 4, 2, 32, 1024], P('pair', 'win')
- send_blocks: int32 [64, 64, 2], P('pair'), may hold values from 0 to 7, as said below
- tile_slots: int32 [256, 2], P('pair'), may hold values from 0 to 127, as said below
Outputs:
- correlations: bfloat16 [32, 256, 32, 1024], P('win', 'pair')
The draws below stay inside these ranges and needn't reach their ends.
Inputs may be any that keep to these rules, and one draw needn't show every extreme that they name: `send_blocks`: entry [s, d, k] names the block, counted within pair index s, that s sends to owner d in slot k; the 2 slots of one s and d name different blocks. `tile_slots`: row t belongs to owner t // 4; an entry r stands for slot r % 2 of what pair index r // 2 sends to that owner. The second entry of a row lies 1 to 2 slots after or before the first, so the two blocks of a tile are different and lie on the same or neighbouring pair indices.
All inputs are finite; a program needn't handle non-finite values.
Results may differ from the reference program's by a relative error of at most 0.0068.
Values may be sent and summed in bfloat16 or wider, within the bound.
No kernel may reach another device: no remote copies, remote signals or barrier semaphores. Data moves between devices by JAX's collectives and lax.ppermute only.
A program may use at most 320 MiB of HBM per device.

```python
import math
import jax
import jax.numpy as jnp
from jax import lax

F = 1024
LAGS = 1024
NS = 4096
F0 = 64
BAND = 64
BC = 32
CAP = 2
NB_DEV = 8
TD = 4
NB = 512
NW = 4
TILES = 256


def draw_spectra(key, part):
    key = jax.random.fold_in(key, 11)
    base_key, row_key, column_key = jax.random.split(key, 3)
    whole_shape = (NB, NW, 2, BC, F)
    base = jax.random.normal(base_key, whole_shape, jnp.float32)
    row_top = math.log(10.0)
    row_scale = jnp.exp(jax.random.uniform(row_key, (NB, NW, 1, BC, 1), jnp.float32, 0.0, row_top))
    column_scale = jnp.exp(jax.random.uniform(column_key, (1, 1, 1, 1, F), jnp.float32, 0.0, math.log(10.0)))
    return (base * row_scale * column_scale).astype(jnp.bfloat16)


def draw_send_blocks(key, part):
    key = jax.random.fold_in(key, 37)
    owners = NB // NB_DEV
    scores = jax.random.randint(key, (owners, owners, NB_DEV), 0, 1 << 20, dtype=jnp.int32)
    scores = scores * NB_DEV + jnp.arange(NB_DEV, dtype=jnp.int32)
    ordered = jnp.argsort(scores, axis=-1, stable=True)[..., :CAP].astype(jnp.int32)
    spread = jnp.arange(CAP, dtype=jnp.int32) * (NB_DEV - 1) // max(CAP - 1, 1)
    ordered = ordered.at[:, 0, :].set(spread)
    return ordered.astype(jnp.int32)


def draw_tile_slots(key, part):
    key = jax.random.fold_in(key, 23)
    owners = TILES // TD
    slot_total = owners * CAP
    owner_keys = jax.random.split(key, owners)

    def one_owner(owner_key):
        order_key, step_key = jax.random.split(owner_key)
        shuffled = jax.random.permutation(order_key, slot_total).astype(jnp.int32)
        first_slot = shuffled[jnp.arange(TD, dtype=jnp.int32) % slot_total]
        first_slot = first_slot.at[0].set(slot_total - 1).at[1].set(0)
        step_size = jax.random.randint(step_key, (TD,), 1, CAP + 1, dtype=jnp.int32)
        second_slot = jnp.where(first_slot + step_size < slot_total, first_slot + step_size, first_slot - step_size)
        return jnp.stack([first_slot, second_slot], axis=1).astype(jnp.int32)
    return jax.vmap(one_owner)(owner_keys).reshape(TILES, 2).astype(jnp.int32)


def setup_inputs(seed: int = 0) -> dict:
    arg_keys = jax.random.split(jax.random.key(seed), 4)
    spectra = draw_spectra(jax.random.fold_in(arg_keys[3], 71), 0)
    send_blocks = draw_send_blocks(jax.random.fold_in(arg_keys[3], 71), 0)
    tile_slots = draw_tile_slots(jax.random.fold_in(arg_keys[3], 71), 0)
    return dict(spectra=spectra, send_blocks=send_blocks, tile_slots=tile_slots)


def whiten(spectral):
    whole_shape = spectral.shape
    band_count = whole_shape[-1] // BAND
    widened = spectral.astype(jnp.float32).reshape(whole_shape[:-1] + (band_count, BAND))
    band_power = lax.optimization_barrier(jnp.mean(widened * widened, axis=(-4, -1), keepdims=True))
    return (widened * lax.rsqrt(band_power + 1e-06)).reshape(whole_shape).astype(jnp.bfloat16)

def lag_rows_table():
    bin_index = jnp.arange(F, dtype=jnp.int32) + F0
    lag_index = jnp.arange(LAGS, dtype=jnp.int32) - LAGS // 2
    wrapped = bin_index[:, None] * lag_index[None, :] % NS
    phases = wrapped.astype(jnp.float32) * (2.0 * math.pi / NS)
    return jnp.concatenate([jnp.cos(phases), -jnp.sin(phases)], axis=0).astype(jnp.bfloat16)

def cross_stack(first_rows, second_rows):
    swapped = jnp.stack([first_rows[:, :, 1], -first_rows[:, :, 0]], axis=2)
    paired = jnp.stack([first_rows, swapped], axis=0)
    return jnp.einsum('stwcif,twcjf->itjsf', paired, second_rows)

def reference(spectra, send_blocks, tile_slots):
    white = whiten(spectra)
    lag_rows = lag_rows_table()
    owners = TILES // TD
    slot_table = tile_slots.reshape(owners, TD, 2)
    scaling = 1.0 / math.sqrt(NW * F)

    def per_owner(operands):
        owner, slots = operands
        source = slots // CAP
        within = slots % CAP
        blocks = (source * NB_DEV + send_blocks[source, owner, within]).astype(jnp.int32)
        first_panels = jnp.take(white, blocks[:, 0], axis=0).astype(jnp.float32)
        second_panels = jnp.take(white, blocks[:, 1], axis=0).astype(jnp.float32)
        cross_terms = cross_stack(first_panels, second_panels)
        stacked = cross_terms.astype(jnp.bfloat16)
        lagged = jnp.dot(stacked.reshape(-1, 2 * F), lag_rows, preferred_element_type=jnp.float32) * scaling
        return lagged.reshape(BC, TD, BC, LAGS).astype(jnp.bfloat16)
    per_tile = lax.map(per_owner, (jnp.arange(owners, dtype=jnp.int32), slot_table))
    return jnp.transpose(per_tile, (1, 0, 2, 3, 4)).reshape(BC, TILES, BC, LAGS)
```

```python
import functools
import math

import jax
import jax.numpy as jnp
from jax import lax
from jax.experimental import pallas as pl
from jax.experimental.pallas import tpu as pltpu
from jax.sharding import PartitionSpec as P

LAGS = 1024
NS = 4096
F0 = 64
BAND = 64
LANES = 128
GROUP = 8


def whiten_kernel(x_ref, out_ref):
    blocks, bins = x_ref.shape[0], x_ref.shape[-1]
    lane_groups = bins // LANES
    row_band = lax.broadcasted_iota(jnp.int32, (LANES, LANES), 0) // BAND
    column_band = lax.broadcasted_iota(jnp.int32, (LANES, LANES), 1) // BAND
    ones = jnp.where(row_band == column_band, 1.0 / (2 * BAND), 0.0).astype(jnp.float32)
    for block in range(blocks):
        for lane_group in range(lane_groups):
            lanes = slice(lane_group * LANES, (lane_group + 1) * LANES)
            real = x_ref[block, 0, 0, :, lanes].astype(jnp.float32)
            imag = x_ref[block, 0, 1, :, lanes].astype(jnp.float32)
            power = jnp.dot(
                real * real + imag * imag,
                ones,
                precision=lax.Precision.HIGHEST,
                preferred_element_type=jnp.float32,
            )
            scale = lax.rsqrt(power + 1e-06)
            for part, rows in enumerate((real * scale, imag * scale)):
                for half in range(2):
                    piece = rows[half * GROUP : (half + 1) * GROUP].astype(jnp.bfloat16)
                    out_ref[(half * 2 + part) * lane_groups + lane_group, block] = piece


def whiten_spread(spectra):
    blocks, _, parts, channels, bins = spectra.shape
    pieces = parts * channels * bins // (GROUP * LANES)
    steps = channels // 16
    return pl.pallas_call(
        whiten_kernel,
        grid=(steps,),
        in_specs=[pl.BlockSpec((blocks, 1, parts, 16, bins), lambda g: (0, 0, 0, g, 0))],
        out_specs=pl.BlockSpec((pieces // steps, blocks, GROUP, LANES), lambda g: (g, 0, 0, 0)),
        out_shape=jax.ShapeDtypeStruct((pieces, blocks, GROUP, LANES), jnp.bfloat16),
        compiler_params=pltpu.CompilerParams(vmem_limit_bytes=24 * 2**20),
        name="whiten_spread",
    )(spectra)


def pick_kernel(index_ref, x_ref, first_ref, second_ref):
    owners, tiles = first_ref.shape[:2]

    def one_owner(owner, carry):
        for tile in range(tiles):
            base = (owner * tiles + tile) * 2
            first_ref[owner, tile] = x_ref[index_ref[base]]
            second_ref[owner, tile] = x_ref[index_ref[base + 1]]
        return carry

    lax.fori_loop(0, owners, one_owner, 0)


def pick(index, spread, owners, tiles):
    shape = jax.ShapeDtypeStruct((owners, tiles, GROUP, LANES), jnp.bfloat16)
    return pl.pallas_call(
        pick_kernel,
        in_specs=[
            pl.BlockSpec(memory_space=pltpu.SMEM),
            pl.BlockSpec(memory_space=pltpu.VMEM),
        ],
        out_specs=[pl.BlockSpec(memory_space=pltpu.VMEM)] * 2,
        out_shape=[shape, shape],
        compiler_params=pltpu.CompilerParams(vmem_limit_bytes=24 * 2**20),
        name="pick_blocks",
    )(index, spread)


def correlate_kernel(scaling, a_ref, b_ref, table_ref, out_ref, stack_ref):
    tile = pl.program_id(0)
    windows, _, lane_groups = a_ref.shape[:3]
    groups = b_ref.shape[1]
    bins = lane_groups * LANES
    channels = groups * GROUP

    def one_lane_group(lane_group, carry):
        lanes = pl.multiple_of(lane_group * LANES, LANES)
        a = [
            [a_ref[w, part, lane_group, tile].astype(jnp.float32) for part in range(2)]
            for w in range(windows)
        ]
        for pair in range(groups // 2):
            b = [
                [
                    [
                        b_ref[w, pair * 2 + half, part, lane_group, tile].astype(jnp.float32)
                        for part in range(2)
                    ]
                    for w in range(windows)
                ]
                for half in range(2)
            ]
            for i in range(GROUP):
                rows = [[None, None], [None, None]]
                for w in range(windows):
                    a0 = jnp.broadcast_to(a[w][0][i : i + 1], (GROUP, LANES))
                    a1 = jnp.broadcast_to(a[w][1][i : i + 1], (GROUP, LANES))
                    for half in range(2):
                        b0, b1 = b[half][w]
                        real = a0 * b0 + a1 * b1
                        imag = a1 * b0 - a0 * b1
                        if w:
                            real += rows[half][0]
                            imag += rows[half][1]
                        rows[half] = [real, imag]
                start = i * channels + pair * 2 * GROUP
                for part in range(2):
                    joined = jnp.concatenate([rows[0][part], rows[1][part]], axis=0)
                    stack_ref[
                        start : start + 2 * GROUP, pl.ds(part * bins + lanes, LANES)
                    ] = joined.astype(jnp.bfloat16)
        return carry

    lax.fori_loop(0, lane_groups, one_lane_group, 0)
    lagged = jnp.dot(stack_ref[...], table_ref[...], preferred_element_type=jnp.float32)
    lagged = (lagged * scaling).astype(jnp.bfloat16)
    out_ref[...] = lagged.reshape(out_ref.shape)


def correlate(a, b, table):
    windows, _, lane_groups, tiles = a.shape[:4]
    channels = b.shape[1] * GROUP
    bins = lane_groups * LANES
    lags = table.shape[1]
    scaling = 1.0 / math.sqrt(windows * bins)
    return pl.pallas_call(
        functools.partial(correlate_kernel, scaling),
        grid=(tiles,),
        in_specs=[
            pl.BlockSpec(a.shape, lambda t: (0,) * 6),
            pl.BlockSpec(b.shape, lambda t: (0,) * 7),
            pl.BlockSpec(table.shape, lambda t: (0, 0)),
        ],
        out_specs=pl.BlockSpec((GROUP, 1, channels, lags), lambda t: (0, t, 0, 0)),
        out_shape=jax.ShapeDtypeStruct((GROUP, tiles, channels, lags), jnp.bfloat16),
        scratch_shapes=[pltpu.VMEM((GROUP * channels, 2 * bins), jnp.bfloat16)],
        compiler_params=pltpu.CompilerParams(vmem_limit_bytes=48 * 2**20),
        name="correlate",
    )(a, b, table)


def lag_rows_table(bin_total):
    bin_index = jnp.arange(bin_total, dtype=jnp.int32) + F0
    lag_index = jnp.arange(LAGS, dtype=jnp.int32) - LAGS // 2
    wrapped = bin_index[:, None] * lag_index[None, :] % NS
    phases = wrapped.astype(jnp.float32) * (2.0 * math.pi / NS)
    return jnp.concatenate([jnp.cos(phases), -jnp.sin(phases)], axis=0).astype(jnp.bfloat16)


def block_index(send_blocks, tile_slots, blocks):
    owners, capacity = send_blocks.shape[1:]
    tiles = tile_slots.shape[0]
    mine = jnp.concatenate([send_blocks.reshape(-1), tile_slots.reshape(-1)])
    tables = lax.all_gather(mine, "pair", axis=0, tiled=False)
    sent = tables[:, : owners * capacity].reshape(owners, owners, capacity)
    slots = tables[:, owners * capacity :]
    sent = sent + blocks * jnp.arange(owners, dtype=jnp.int32)[:, None, None]
    by_owner = jnp.transpose(sent, (1, 0, 2)).reshape(owners, 1, owners * capacity)
    chosen = slots[:, :, None] == jnp.arange(owners * capacity, dtype=jnp.int32)
    return jnp.sum(jnp.where(chosen, by_owner, 0), axis=-1).reshape(owners * tiles * 2)


def local(spectra, send_blocks, tile_slots):
    owners = lax.axis_size("pair")
    windows = lax.axis_size("win")
    blocks, _, parts, channels, bins = spectra.shape
    tiles = tile_slots.shape[0]
    lane_groups = bins // LANES
    index = block_index(send_blocks, tile_slots, blocks)
    outgoing = whiten_spread(spectra)
    spread = lax.all_to_all(outgoing, "pair", split_axis=0, concat_axis=0, tiled=True)
    spread = spread.reshape(owners * blocks, GROUP, LANES)
    first, second = pick(index, spread, owners, tiles)
    second = lax.all_to_all(second, "pair", split_axis=0, concat_axis=0, tiled=True)
    all_second = lax.all_gather(second, "win", axis=0, tiled=False)
    first = lax.all_to_all(first, "pair", split_axis=0, concat_axis=0, tiled=True)
    all_first = lax.all_to_all(first, "win", split_axis=0, concat_axis=0, tiled=True)
    a = all_first.reshape(windows, parts, lane_groups, tiles, GROUP, LANES)
    b = all_second.reshape(windows, channels // GROUP, parts, lane_groups, tiles, GROUP, LANES)
    return correlate(a, b, lag_rows_table(bins))


def solution(mesh):
    in_specs = (P("pair", "win", None, None, None), P("pair", None, None), P("pair", None))
    out_specs = P("win", "pair", None, None)
    return jax.shard_map(local, mesh=mesh, in_specs=in_specs, out_specs=out_specs, check_vma=False)
```

```python
import functools
import math

import jax
import jax.numpy as jnp
from jax import lax
from jax.experimental import pallas as pl
from jax.experimental.pallas import tpu as pltpu
from jax.sharding import PartitionSpec as P

LAGS = 1024
NS = 4096
F0 = 64
BAND = 64
LANES = 128
GROUP = 8
HALF = 64


def whiten_kernel(x_ref, sent_ref, slots_ref, out_ref, table_ref):
    blocks, bins = x_ref.shape[0], x_ref.shape[-1]
    lane_groups = bins // LANES
    row_band = lax.broadcasted_iota(jnp.int32, (LANES, LANES), 0) // BAND
    column_band = lax.broadcasted_iota(jnp.int32, (LANES, LANES), 1) // BAND
    ones = jnp.where(row_band == column_band, 1.0, 0.0).astype(jnp.bfloat16)
    ones = jnp.concatenate([ones, ones, ones], axis=0)
    for lane_group in range(lane_groups):
        lanes = slice(lane_group * LANES, (lane_group + 1) * LANES)
        real = x_ref[:, 0, 0, :, lanes].astype(jnp.float32).reshape(blocks * 16, LANES)
        imag = x_ref[:, 0, 1, :, lanes].astype(jnp.float32).reshape(blocks * 16, LANES)
        rest = real * real + imag * imag
        terms = []
        for _ in range(3):
            terms.append(rest.astype(jnp.bfloat16))
            rest = rest - terms[-1].astype(jnp.float32)
        power = jnp.dot(jnp.concatenate(terms, axis=1), ones, preferred_element_type=jnp.float32)
        scale = lax.rsqrt(power * (1.0 / (2 * BAND)) + 1e-06)
        for part, rows in enumerate((real * scale, imag * scale)):
            rows = rows.reshape(blocks, 2, GROUP, LANES)
            for half in range(2):
                place = (half * 2 + part) * lane_groups + lane_group
                out_ref[place, :blocks] = rows[:, half].astype(jnp.bfloat16)
    table_ref[...] = jnp.zeros_like(table_ref)
    table_ref[0:2, : sent_ref.shape[1]] = sent_ref[...].astype(jnp.float32)
    table_ref[2:4, : slots_ref.shape[1]] = slots_ref[...].astype(jnp.float32)
    piece = table_ref[...].astype(jnp.bfloat16)
    out_ref[:, blocks] = jnp.broadcast_to(piece, (out_ref.shape[0],) + piece.shape)


def whiten_spread(spectra, sent, slots):
    blocks, _, parts, channels, bins = spectra.shape
    pieces = parts * channels * bins // (GROUP * LANES)
    steps = channels // 16
    return pl.pallas_call(
        whiten_kernel,
        grid=(steps,),
        in_specs=[
            pl.BlockSpec((blocks, 1, parts, 16, bins), lambda g: (0, 0, 0, g, 0)),
            pl.BlockSpec(sent.shape, lambda g: (0, 0)),
            pl.BlockSpec(slots.shape, lambda g: (0, 0)),
        ],
        out_specs=pl.BlockSpec((pieces // steps, blocks + 1, GROUP, LANES), lambda g: (g, 0, 0, 0)),
        out_shape=jax.ShapeDtypeStruct((pieces, blocks + 1, GROUP, LANES), jnp.bfloat16),
        scratch_shapes=[pltpu.VMEM((GROUP, LANES), jnp.float32)],
        compiler_params=pltpu.CompilerParams(vmem_limit_bytes=24 * 2**20),
        name="whiten_spread",
    )(spectra, sent, slots)


def pick_kernel(x_ref, *refs):
    out_refs, (table_ref, index_ref, place_ref, sem) = refs[:-4], refs[-4:]
    owners, stride = x_ref.shape[:2]
    table_ref[...] = x_ref[:, stride - 1].astype(jnp.float32).reshape(table_ref.shape)
    sent = [table_ref[pl.ds(k, owners, stride=GROUP), :] for k in range(2)]
    lane = lax.broadcasted_iota(jnp.int32, (owners, LANES), 1)
    by_owner = jnp.concatenate(sent, axis=0).T[:owners].astype(jnp.int32)
    by_owner = by_owner + stride * (lane % HALF)
    places = jnp.zeros((owners, LANES), jnp.int32)
    tiles = sum(ref.shape[1] for ref in out_refs) // 2
    for part in range(2):
        slots = table_ref[pl.ds(2 + part, owners, stride=GROUP), :].astype(jnp.int32)
        for tile in range(tiles):
            slot = slots[:, tile : tile + 1]
            hit = lane == (slot % 2) * HALF + slot // 2
            place = jnp.sum(jnp.where(hit, by_owner, 0), axis=1, keepdims=True)
            places = jnp.where(lane == part * tiles + tile, place, places)
    index_ref[...] = places
    copy = pltpu.make_async_copy(index_ref, place_ref, sem)
    copy.start()
    copy.wait()
    flat = x_ref.reshape(owners * stride, GROUP, LANES)

    def one_owner(owner, carry):
        start = 0
        for out_ref in out_refs:
            count = out_ref.shape[1] // 2
            for part in range(2):
                for tile in range(count):
                    place = place_ref[owner, part * tiles + start + tile]
                    out_ref[owner, part * count + tile] = flat[place]
            start += count
        return carry

    lax.fori_loop(0, owners, one_owner, 0, unroll=2)


def pick(spread, shares):
    owners = spread.shape[0]
    shapes = [
        jax.ShapeDtypeStruct((owners, 2 * count, GROUP, LANES), jnp.bfloat16) for count in shares
    ]
    return pl.pallas_call(
        pick_kernel,
        in_specs=[pl.BlockSpec(memory_space=pltpu.VMEM)],
        out_specs=[pl.BlockSpec(memory_space=pltpu.VMEM)] * len(shapes),
        out_shape=shapes,
        scratch_shapes=[
            pltpu.VMEM((owners * GROUP, LANES), jnp.float32),
            pltpu.VMEM((owners, LANES), jnp.int32),
            pltpu.SMEM((owners, LANES), jnp.int32),
            pltpu.SemaphoreType.DMA,
        ],
        compiler_params=pltpu.CompilerParams(vmem_limit_bytes=24 * 2**20),
        name="pick_blocks",
    )(spread)


def correlate_kernel(scaling, windows, win_ref, a_ref, *refs):
    b_refs, table_ref = refs[:windows], refs[windows]
    out_ref, stack_ref = refs[-2:]
    step = pl.program_id(0)
    last = pl.num_programs(0) - 1
    lane_groups = a_ref.shape[2]
    groups = b_refs[0].shape[0]
    bins = lane_groups * LANES
    channels = groups * GROUP
    source = [lax.rem(win_ref[0] + windows - w, windows) for w in range(windows)]

    def cross(lane_group, slot):
        lanes = pl.multiple_of(lane_group * LANES, LANES)
        a = [
            [a_ref[source[w], part, lane_group, step].astype(jnp.float32) for part in range(2)]
            for w in range(windows)
        ]
        for pair in range(groups // 2):
            b = [
                [
                    [
                        b_refs[w][pair * 2 + half, part, lane_group, step].astype(jnp.float32)
                        for part in range(2)
                    ]
                    for w in range(windows)
                ]
                for half in range(2)
            ]
            for i in range(GROUP):
                rows = [[None, None], [None, None]]
                for w in range(windows):
                    a0 = jnp.broadcast_to(a[w][0][i : i + 1], (GROUP, LANES))
                    a1 = jnp.broadcast_to(a[w][1][i : i + 1], (GROUP, LANES))
                    for half in range(2):
                        b0, b1 = b[half][w]
                        real = a0 * b0 + a1 * b1
                        imag = a1 * b0 - a0 * b1
                        if w:
                            real += rows[half][0]
                            imag += rows[half][1]
                        rows[half] = [real, imag]
                start = i * channels + pair * 2 * GROUP
                for part in range(2):
                    joined = jnp.concatenate([rows[0][part], rows[1][part]], axis=0)
                    stack_ref[
                        slot, start : start + 2 * GROUP, pl.ds(part * bins + lanes, LANES)
                    ] = joined.astype(jnp.bfloat16)

    def lagged(chunk, slot):
        columns = pl.ds(pl.multiple_of(chunk * 2 * LANES, 2 * LANES), 2 * LANES)
        rows = jnp.dot(stack_ref[slot], table_ref[:, columns], preferred_element_type=jnp.float32)
        rows = (rows * scaling).astype(jnp.bfloat16)
        out_ref[:, 0, :, columns] = rows.reshape(GROUP, channels, 2 * LANES)

    def run(with_cross, with_lagged):
        def body(chunk, carry):
            if with_lagged:
                lagged(chunk, lax.rem(step + 1, 2))
            if with_cross:
                cross(chunk * 2, lax.rem(step, 2))
                cross(chunk * 2 + 1, lax.rem(step, 2))
            return carry

        lax.fori_loop(0, lane_groups // 2, body, 0)

    @pl.when(step == 0)
    def _():
        run(True, False)

    @pl.when(jnp.logical_and(step > 0, step < last))
    def _():
        run(True, True)

    @pl.when(step == last)
    def _():
        run(False, True)


def correlate(a, b, table, start, tiles, result):
    windows, _, lane_groups, count = a.shape[:4]
    channels = b[0].shape[0] * GROUP
    bins = lane_groups * LANES
    lags = table.shape[1]
    scaling = 1.0 / math.sqrt(windows * bins)
    win = lax.axis_index("win").astype(jnp.int32).reshape(1)
    whole = lambda x: pl.BlockSpec(x.shape, lambda t: (0,) * len(x.shape))
    operands = [win, a, *b, table]
    in_specs = [pl.BlockSpec(memory_space=pltpu.SMEM)] + [whole(x) for x in operands[1:]]
    aliases = {}
    if result is not None:
        aliases = {len(operands): 0}
        operands.append(result)
        in_specs.append(pl.BlockSpec(memory_space=pl.ANY))
    place = lambda t: (0, start + jnp.maximum(t - 1, 0), 0, 0)
    return pl.pallas_call(
        functools.partial(correlate_kernel, scaling, windows),
        grid=(count + 1,),
        in_specs=in_specs,
        out_specs=pl.BlockSpec((GROUP, 1, channels, lags), place),
        out_shape=jax.ShapeDtypeStruct((GROUP, tiles, channels, lags), jnp.bfloat16),
        scratch_shapes=[pltpu.VMEM((2, GROUP * channels, 2 * bins), jnp.bfloat16)],
        input_output_aliases=aliases,
        compiler_params=pltpu.CompilerParams(vmem_limit_bytes=40 * 2**20),
        cost_estimate=pl.CostEstimate(
            flops=4 * count * GROUP * channels * bins * lags,
            bytes_accessed=8 * 2**20,
            transcendentals=0,
        ),
        name="correlate",
    )(*operands)


def lag_rows_table(bin_total):
    bin_index = jnp.arange(bin_total, dtype=jnp.int32) + F0
    lag_index = jnp.arange(LAGS, dtype=jnp.int32) - LAGS // 2
    wrapped = bin_index[:, None] * lag_index[None, :] % NS
    phases = wrapped.astype(jnp.float32) * (2.0 * math.pi / NS)
    return jnp.concatenate([jnp.cos(phases), -jnp.sin(phases)], axis=0).astype(jnp.bfloat16)


def local(spectra, send_blocks, tile_slots):
    windows = lax.axis_size("win")
    blocks, _, parts, channels, bins = spectra.shape
    tiles = tile_slots.shape[0]
    lane_groups = bins // LANES
    shares = (tiles // 2, tiles - tiles // 2)
    exchange = lambda x, axis: lax.all_to_all(x, axis, split_axis=0, concat_axis=0, tiled=True)

    outgoing = whiten_spread(spectra, send_blocks[0].T, tile_slots.T)
    spread = exchange(outgoing, "pair")
    spread, table = lax.optimization_barrier((spread, lag_rows_table(bins)))
    picked = pick(spread, shares)
    result, start = None, 0
    for share, count in enumerate(shares):
        both = exchange(picked[share], "pair")
        first, second = both[:, :count], both[:, count:]
        a = exchange(first, "win").reshape(windows, parts, lane_groups, count, GROUP, LANES)
        b = [second]
        for distance in range(1, windows):
            turn = [(w, (w + distance) % windows) for w in range(windows)]
            b.append(lax.ppermute(second, "win", turn))
        b = [x.reshape(channels // GROUP, parts, lane_groups, count, GROUP, LANES) for x in b]
        result = correlate(a, b, table, start, tiles, result)
        start += count
    return result


def solution(mesh):
    in_specs = (P("pair", "win", None, None, None), P("pair", None, None), P("pair", None))
    out_specs = P("win", "pair", None, None)
    return jax.shard_map(local, mesh=mesh, in_specs=in_specs, out_specs=out_specs, check_vma=False)
```

```python
import functools
import math

import jax
import jax.numpy as jnp
from jax import lax
from jax.experimental import pallas as pl
from jax.experimental.pallas import tpu as pltpu
from jax.sharding import PartitionSpec as P

LAGS = 1024
NS = 4096
F0 = 64
BAND = 64
LANES = 128
GROUP = 8
HALF = 64


def whiten_kernel(win_ref, x_ref, sent_ref, slots_ref, out_ref, table_ref):
    blocks = x_ref.shape[0]
    _, lane_groups, groups = out_ref.shape[:3]
    step = pl.program_id(0)
    row_band = lax.broadcasted_iota(jnp.int32, (LANES, LANES), 0) // BAND
    column_band = lax.broadcasted_iota(jnp.int32, (LANES, LANES), 1) // BAND
    ones = jnp.where(row_band == column_band, 1.0, 0.0).astype(jnp.bfloat16)
    ones = jnp.concatenate([ones, ones, ones], axis=0)
    for lane_group in range(lane_groups):
        lanes = slice(lane_group * LANES, (lane_group + 1) * LANES)
        real = x_ref[:, 0, 0, :, lanes].astype(jnp.float32).reshape(blocks * 16, LANES)
        imag = x_ref[:, 0, 1, :, lanes].astype(jnp.float32).reshape(blocks * 16, LANES)
        rest = real * real + imag * imag
        terms = []
        for _ in range(3):
            terms.append(rest.astype(jnp.bfloat16))
            rest = rest - terms[-1].astype(jnp.float32)
        power = jnp.dot(jnp.concatenate(terms, axis=1), ones, preferred_element_type=jnp.float32)
        scale = lax.rsqrt(power * (1.0 / (2 * BAND)) + 1e-06)
        for part, rows in enumerate((real * scale, imag * scale)):
            rows = rows.reshape(blocks, 2, GROUP, LANES)
            for half in range(2):
                place = lax.rem(2 * step + half + groups - win_ref[0], groups)
                out_ref[part, lane_group, place, :blocks] = rows[:, half].astype(jnp.bfloat16)

    @pl.when(step == 0)
    def _():
        table_ref[...] = jnp.zeros_like(table_ref)
        table_ref[0:2, : sent_ref.shape[1]] = sent_ref[...].astype(jnp.float32)
        table_ref[2:4, : slots_ref.shape[1]] = slots_ref[...].astype(jnp.float32)
        piece = table_ref[...].astype(jnp.bfloat16)
        shape = out_ref.shape
        out_ref[:, :, :, blocks] = jnp.broadcast_to(piece, shape[:3] + shape[4:])


def whiten_spread(win, spectra, sent, slots):
    blocks, _, parts, channels, bins = spectra.shape
    shape = (parts, bins // LANES, channels // GROUP, blocks + 1, GROUP, LANES)
    return pl.pallas_call(
        whiten_kernel,
        grid=(channels // 16,),
        in_specs=[
            pl.BlockSpec(memory_space=pltpu.SMEM),
            pl.BlockSpec((blocks, 1, parts, 16, bins), lambda g: (0, 0, 0, g, 0)),
            pl.BlockSpec(sent.shape, lambda g: (0, 0)),
            pl.BlockSpec(slots.shape, lambda g: (0, 0)),
        ],
        out_specs=pl.BlockSpec(shape, lambda g: (0,) * len(shape)),
        out_shape=jax.ShapeDtypeStruct(shape, jnp.bfloat16),
        scratch_shapes=[pltpu.VMEM((GROUP, LANES), jnp.float32)],
        compiler_params=pltpu.CompilerParams(vmem_limit_bytes=60 * 2**20),
        name="whiten_spread",
    )(win, spectra, sent, slots)


def copy_pieces(place_ref, x_ref, out_ref, start):
    flat = x_ref.reshape((x_ref.shape[0] * x_ref.shape[1],) + x_ref.shape[2:])

    def one_owner(owner, carry):
        for tile in range(out_ref.shape[1]):
            out_ref[owner, tile] = flat[place_ref[owner, start + tile]]
        return carry

    lax.fori_loop(0, out_ref.shape[0], one_owner, 0, unroll=4)


def pick_second_kernel(x_ref, out_ref, index_ref, table_ref, place_ref, sem):
    owners, stride = x_ref.shape[:2]
    tiles = out_ref.shape[1]
    table_ref[...] = x_ref[:, stride - 1].astype(jnp.float32).reshape(table_ref.shape)
    sent = [table_ref[pl.ds(k, owners, stride=GROUP), :] for k in range(2)]
    lane = lax.broadcasted_iota(jnp.int32, (owners, LANES), 1)
    by_owner = jnp.concatenate(sent, axis=0).T[:owners].astype(jnp.int32)
    by_owner = by_owner + stride * (lane % HALF)
    places = jnp.zeros((owners, LANES), jnp.int32)
    for part in range(2):
        slots = table_ref[pl.ds(2 + part, owners, stride=GROUP), :].astype(jnp.int32)
        for tile in range(tiles):
            slot = slots[:, tile : tile + 1]
            hit = lane == (slot % 2) * HALF + slot // 2
            place = jnp.sum(jnp.where(hit, by_owner, 0), axis=1, keepdims=True)
            places = jnp.where(lane == part * tiles + tile, place, places)
    index_ref[...] = places
    copy = pltpu.make_async_copy(index_ref, place_ref, sem)
    copy.start()
    copy.wait()
    copy_pieces(place_ref, x_ref, out_ref, tiles)


def pick_second(spread, tiles):
    owners = spread.shape[0]
    return pl.pallas_call(
        pick_second_kernel,
        in_specs=[pl.BlockSpec(memory_space=pltpu.VMEM)],
        out_specs=[pl.BlockSpec(memory_space=pltpu.VMEM)] * 2,
        out_shape=[
            jax.ShapeDtypeStruct((owners, tiles, GROUP, LANES), jnp.bfloat16),
            jax.ShapeDtypeStruct((owners, LANES), jnp.int32),
        ],
        scratch_shapes=[
            pltpu.VMEM((owners * GROUP, LANES), jnp.float32),
            pltpu.SMEM((owners, LANES), jnp.int32),
            pltpu.SemaphoreType.DMA,
        ],
        compiler_params=pltpu.CompilerParams(vmem_limit_bytes=24 * 2**20),
        name="pick_second",
    )(spread)


def pick_first(index, spread, tiles):
    owners = spread.shape[0]
    return pl.pallas_call(
        lambda place_ref, x_ref, out_ref: copy_pieces(place_ref, x_ref, out_ref, 0),
        in_specs=[
            pl.BlockSpec(memory_space=pltpu.SMEM),
            pl.BlockSpec(memory_space=pltpu.VMEM),
        ],
        out_specs=pl.BlockSpec(memory_space=pltpu.VMEM),
        out_shape=jax.ShapeDtypeStruct((owners, tiles, GROUP, LANES), jnp.bfloat16),
        compiler_params=pltpu.CompilerParams(vmem_limit_bytes=24 * 2**20),
        name="pick_first",
    )(index, spread)


def correlate_kernel(scaling, win_ref, a_ref, *refs):
    windows = a_ref.shape[2]
    b_refs, table_hbm = refs[:windows], refs[windows]
    out_ref, stack_ref, table_ref, sem = refs[windows + 1 :]
    step = pl.program_id(0)
    last = pl.num_programs(0) - 1
    _, lane_groups, groups = b_refs[0].shape[:3]
    bins = lane_groups * LANES
    channels = groups * GROUP
    places = [
        [lax.rem(group + distance + groups - win_ref[0], groups) for group in range(groups)]
        for distance in range(windows)
    ]
    table_copy = pltpu.make_async_copy(table_hbm, table_ref, sem)

    def cross(lane_group, slot):
        lanes = pl.multiple_of(lane_group * LANES, LANES)
        a = [
            [a_ref[part, lane_group, w, step].astype(jnp.float32) for part in range(2)]
            for w in range(windows)
        ]
        for pair in range(groups // 2):
            b = [
                [
                    [
                        b_refs[w][part, lane_group, places[w][pair * 2 + half], step].astype(
                            jnp.float32
                        )
                        for part in range(2)
                    ]
                    for w in range(windows)
                ]
                for half in range(2)
            ]
            for i in range(GROUP):
                rows = [[None, None], [None, None]]
                for w in range(windows):
                    a0 = jnp.broadcast_to(a[w][0][i : i + 1], (GROUP, LANES))
                    a1 = jnp.broadcast_to(a[w][1][i : i + 1], (GROUP, LANES))
                    for half in range(2):
                        b0, b1 = b[half][w]
                        real = a0 * b0 + a1 * b1
                        imag = a1 * b0 - a0 * b1
                        if w:
                            real += rows[half][0]
                            imag += rows[half][1]
                        rows[half] = [real, imag]
                start = i * channels + pair * 2 * GROUP
                for part in range(2):
                    joined = jnp.concatenate([rows[0][part], rows[1][part]], axis=0)
                    stack_ref[
                        slot, start : start + 2 * GROUP, pl.ds(part * bins + lanes, LANES)
                    ] = joined.astype(jnp.bfloat16)

    def lagged(chunk, slot):
        columns = pl.ds(pl.multiple_of(chunk * 2 * LANES, 2 * LANES), 2 * LANES)
        rows = jnp.dot(stack_ref[slot], table_ref[:, columns], preferred_element_type=jnp.float32)
        rows = (rows * scaling).astype(jnp.bfloat16)
        out_ref[:, 0, :, columns] = rows.reshape(GROUP, channels, 2 * LANES)

    def run(with_cross, with_lagged):
        def body(chunk, carry):
            if with_lagged:
                lagged(chunk, lax.rem(step + 1, 2))
            if with_cross:
                cross(chunk * 2, lax.rem(step, 2))
                cross(chunk * 2 + 1, lax.rem(step, 2))
            return carry

        lax.fori_loop(0, lane_groups // 2, body, 0)

    @pl.when(step == 0)
    def _():
        table_copy.start()
        run(True, False)
        table_copy.wait()

    @pl.when(jnp.logical_and(step > 0, step < last))
    def _():
        run(True, True)

    @pl.when(step == last)
    def _():
        run(False, True)


def correlate(win, a, b, table):
    _, lane_groups, windows, tiles = a.shape[:4]
    channels = b[0].shape[2] * GROUP
    bins = lane_groups * LANES
    lags = table.shape[1]
    scaling = 1.0 / math.sqrt(windows * bins)
    whole = lambda x: pl.BlockSpec(x.shape, lambda t: (0,) * len(x.shape))
    return pl.pallas_call(
        functools.partial(correlate_kernel, scaling),
        grid=(tiles + 1,),
        in_specs=[pl.BlockSpec(memory_space=pltpu.SMEM)]
        + [whole(x) for x in (a, *b)]
        + [pl.BlockSpec(memory_space=pltpu.HBM)],
        out_specs=pl.BlockSpec(
            (GROUP, 1, channels, lags), lambda t: (0, jnp.maximum(t - 1, 0), 0, 0)
        ),
        out_shape=jax.ShapeDtypeStruct((GROUP, tiles, channels, lags), jnp.bfloat16),
        scratch_shapes=[
            pltpu.VMEM((2, GROUP * channels, 2 * bins), jnp.bfloat16),
            pltpu.VMEM(table.shape, table.dtype),
            pltpu.SemaphoreType.DMA,
        ],
        compiler_params=pltpu.CompilerParams(vmem_limit_bytes=58 * 2**20),
        name="correlate",
    )(win, a, *b, table)


def lag_rows_table(bin_total):
    bin_index = jnp.arange(bin_total, dtype=jnp.int32) + F0
    lag_index = jnp.arange(LAGS, dtype=jnp.int32) - LAGS // 2
    wrapped = bin_index[:, None] * lag_index[None, :] % NS
    phases = wrapped.astype(jnp.float32) * (2.0 * math.pi / NS)
    return jnp.concatenate([jnp.cos(phases), -jnp.sin(phases)], axis=0).astype(jnp.bfloat16)


def local(spectra, send_blocks, tile_slots):
    windows, owners = lax.axis_size("win"), lax.axis_size("pair")
    blocks, _, parts, channels, bins = spectra.shape
    tiles = tile_slots.shape[0]
    groups = channels // GROUP
    exchange = lambda x: lax.all_to_all(x, "pair", split_axis=0, concat_axis=0, tiled=True)
    pieces = (parts, bins // LANES, groups, tiles, GROUP, LANES)

    win = lax.axis_index("win").astype(jnp.int32).reshape(1)
    outgoing = whiten_spread(win, spectra, send_blocks[0].T, tile_slots.T)
    spread = exchange(outgoing.reshape(owners, blocks + 1, GROUP, LANES))
    spread, table = lax.optimization_barrier((spread, lag_rows_table(bins)))
    second, index = pick_second(spread, tiles)
    first = pick_first(index, spread, tiles)
    turn = [
        (w * owners + j, (w + j) % windows * owners + j)
        for w in range(windows)
        for j in range(owners)
    ]
    first = lax.ppermute(first, ("win", "pair"), turn)
    second = exchange(second)
    second, first = lax.optimization_barrier((second, first))
    b = [second]
    for distance in range(1, windows):
        step = [(w, (w + distance) % windows) for w in range(windows)]
        b.append(lax.ppermute(second, "win", step))
    a = exchange(first).reshape(pieces)
    return correlate(win, a, [x.reshape(pieces) for x in b], table)


def solution(mesh):
    in_specs = (P("pair", "win", None, None, None), P("pair", None, None), P("pair", None))
    out_specs = P("win", "pair", None, None)
    return jax.shard_map(local, mesh=mesh, in_specs=in_specs, out_specs=out_specs, check_vma=False)
```

```python
import functools
import math

import jax
import jax.numpy as jnp
from jax import lax
from jax.experimental import pallas as pl
from jax.experimental.pallas import tpu as pltpu
from jax.sharding import PartitionSpec as P

LAGS = 1024
NS = 4096
F0 = 64
BAND = 64
LANES = 128
GROUP = 8
HALF = 64


def whiten_kernel(win_ref, x_ref, sent_ref, slots_ref, out_ref, table_ref):
    blocks = x_ref.shape[0]
    _, lane_groups, groups = out_ref.shape[:3]
    step = pl.program_id(0)
    row_band = lax.broadcasted_iota(jnp.int32, (LANES, LANES), 0) // BAND
    column_band = lax.broadcasted_iota(jnp.int32, (LANES, LANES), 1) // BAND
    ones = jnp.where(row_band == column_band, 1.0, 0.0).astype(jnp.bfloat16)
    ones = jnp.concatenate([ones, ones, ones], axis=0)
    for lane_group in range(lane_groups):
        lanes = slice(lane_group * LANES, (lane_group + 1) * LANES)
        real = x_ref[:, 0, 0, :, lanes].astype(jnp.float32).reshape(blocks * 16, LANES)
        imag = x_ref[:, 0, 1, :, lanes].astype(jnp.float32).reshape(blocks * 16, LANES)
        rest = real * real + imag * imag
        terms = []
        for _ in range(3):
            terms.append(rest.astype(jnp.bfloat16))
            rest = rest - terms[-1].astype(jnp.float32)
        power = jnp.dot(jnp.concatenate(terms, axis=1), ones, preferred_element_type=jnp.float32)
        scale = lax.rsqrt(power * (1.0 / (2 * BAND)) + 1e-06)
        for part, rows in enumerate((real * scale, imag * scale)):
            rows = rows.reshape(blocks, 2, GROUP, LANES)
            for half in range(2):
                place = lax.rem(2 * step + half + groups - win_ref[0], groups)
                out_ref[part, lane_group, place, :blocks] = rows[:, half].astype(jnp.bfloat16)

    @pl.when(step == 0)
    def _():
        table_ref[...] = jnp.zeros_like(table_ref)
        table_ref[0:2, : sent_ref.shape[1]] = sent_ref[...].astype(jnp.float32)
        table_ref[2:4, : slots_ref.shape[1]] = slots_ref[...].astype(jnp.float32)
        piece = table_ref[...].astype(jnp.bfloat16)
        shape = out_ref.shape
        out_ref[:, :, :, blocks] = jnp.broadcast_to(piece, shape[:3] + shape[4:])


def whiten_spread(win, spectra, sent, slots):
    blocks, _, parts, channels, bins = spectra.shape
    shape = (parts, bins // LANES, channels // GROUP, blocks + 1, GROUP, LANES)
    return pl.pallas_call(
        whiten_kernel,
        grid=(channels // 16,),
        in_specs=[
            pl.BlockSpec(memory_space=pltpu.SMEM),
            pl.BlockSpec((blocks, 1, parts, 16, bins), lambda g: (0, 0, 0, g, 0)),
            pl.BlockSpec(sent.shape, lambda g: (0, 0)),
            pl.BlockSpec(slots.shape, lambda g: (0, 0)),
        ],
        out_specs=pl.BlockSpec(shape, lambda g: (0,) * len(shape)),
        out_shape=jax.ShapeDtypeStruct(shape, jnp.bfloat16),
        scratch_shapes=[pltpu.VMEM((GROUP, LANES), jnp.float32)],
        compiler_params=pltpu.CompilerParams(vmem_limit_bytes=60 * 2**20),
        name="whiten_spread",
    )(win, spectra, sent, slots)


def copy_pieces(place_ref, x_ref, out_ref, start):
    flat = x_ref.reshape((x_ref.shape[0] * x_ref.shape[1],) + x_ref.shape[2:])

    def one_owner(owner, carry):
        for tile in range(out_ref.shape[1]):
            out_ref[owner, tile] = flat[place_ref[owner, start + tile]]
        return carry

    lax.fori_loop(0, out_ref.shape[0], one_owner, 0, unroll=4)


def pick_second_kernel(x_ref, out_ref, index_ref, table_ref, place_ref, sem):
    owners, stride = x_ref.shape[:2]
    tiles = out_ref.shape[1]
    table_ref[...] = x_ref[:, stride - 1].astype(jnp.float32).reshape(table_ref.shape)
    sent = [table_ref[pl.ds(k, owners, stride=GROUP), :] for k in range(2)]
    lane = lax.broadcasted_iota(jnp.int32, (owners, LANES), 1)
    by_owner = jnp.concatenate(sent, axis=0).T[:owners].astype(jnp.int32)
    by_owner = by_owner + stride * (lane % HALF)
    places = jnp.zeros((owners, LANES), jnp.int32)
    for part in range(2):
        slots = table_ref[pl.ds(2 + part, owners, stride=GROUP), :].astype(jnp.int32)
        for tile in range(tiles):
            slot = slots[:, tile : tile + 1]
            hit = lane == (slot % 2) * HALF + slot // 2
            place = jnp.sum(jnp.where(hit, by_owner, 0), axis=1, keepdims=True)
            places = jnp.where(lane == part * tiles + tile, place, places)
    index_ref[...] = places
    copy = pltpu.make_async_copy(index_ref, place_ref, sem)
    copy.start()
    copy.wait()
    copy_pieces(place_ref, x_ref, out_ref, tiles)


def pick_second(spread, tiles):
    owners = spread.shape[0]
    return pl.pallas_call(
        pick_second_kernel,
        in_specs=[pl.BlockSpec(memory_space=pltpu.VMEM)],
        out_specs=[pl.BlockSpec(memory_space=pltpu.VMEM)] * 2,
        out_shape=[
            jax.ShapeDtypeStruct((owners, tiles, GROUP, LANES), jnp.bfloat16),
            jax.ShapeDtypeStruct((owners, LANES), jnp.int32),
        ],
        scratch_shapes=[
            pltpu.VMEM((owners * GROUP, LANES), jnp.float32),
            pltpu.SMEM((owners, LANES), jnp.int32),
            pltpu.SemaphoreType.DMA,
        ],
        compiler_params=pltpu.CompilerParams(vmem_limit_bytes=24 * 2**20),
        name="pick_second",
    )(spread)


def pick_first(index, spread, tiles):
    owners = spread.shape[0]
    return pl.pallas_call(
        lambda place_ref, x_ref, out_ref: copy_pieces(place_ref, x_ref, out_ref, 0),
        in_specs=[
            pl.BlockSpec(memory_space=pltpu.SMEM),
            pl.BlockSpec(memory_space=pltpu.VMEM),
        ],
        out_specs=pl.BlockSpec(memory_space=pltpu.VMEM),
        out_shape=jax.ShapeDtypeStruct((owners, tiles, GROUP, LANES), jnp.bfloat16),
        compiler_params=pltpu.CompilerParams(vmem_limit_bytes=24 * 2**20),
        name="pick_first",
    )(index, spread)


def correlate_kernel(
    scaling, win_ref, a_ref, b_ref, table_hbm, out_ref, stack_ref, table_ref, sem
):
    step = pl.program_id(0)
    last = pl.num_programs(0) - 1
    windows, _, lane_groups, groups = b_ref.shape[:4]
    bins = lane_groups * LANES
    channels = groups * GROUP
    sources = [lax.rem(win_ref[0] + windows - d, windows) for d in range(windows)]
    places = [
        [lax.rem(group + groups - source, groups) for group in range(groups)]
        for source in sources
    ]
    table_copy = pltpu.make_async_copy(table_hbm, table_ref, sem)

    def cross(lane_group, slot):
        lanes = lane_group * LANES
        a = [
            [a_ref[part, lane_group, w, step].astype(jnp.float32) for part in range(2)]
            for w in range(windows)
        ]
        for pair in range(groups // 2):
            b = [
                [
                    [
                        b_ref[
                            sources[w], part, lane_group, places[w][pair * 2 + half], step
                        ].astype(jnp.float32)
                        for part in range(2)
                    ]
                    for w in range(windows)
                ]
                for half in range(2)
            ]
            for i in range(GROUP):
                rows = [[None, None], [None, None]]
                for w in range(windows):
                    a0 = jnp.broadcast_to(a[w][0][i : i + 1], (GROUP, LANES))
                    a1 = jnp.broadcast_to(a[w][1][i : i + 1], (GROUP, LANES))
                    for half in range(2):
                        b0, b1 = b[half][w]
                        real = a0 * b0 + a1 * b1
                        imag = a1 * b0 - a0 * b1
                        if w:
                            real += rows[half][0]
                            imag += rows[half][1]
                        rows[half] = [real, imag]
                start = i * channels + pair * 2 * GROUP
                for part in range(2):
                    joined = jnp.concatenate([rows[0][part], rows[1][part]], axis=0)
                    stack_ref[
                        slot, start : start + 2 * GROUP, pl.ds(part * bins + lanes, LANES)
                    ] = joined.astype(jnp.bfloat16)

    def lagged(chunk, slot):
        columns = pl.ds(chunk * 2 * LANES, 2 * LANES)
        rows = jnp.dot(stack_ref[slot], table_ref[:, columns], preferred_element_type=jnp.float32)
        rows = (rows * scaling).astype(jnp.bfloat16)
        out_ref[:, 0, :, columns] = rows.reshape(GROUP, channels, 2 * LANES)

    def run(with_cross, with_lagged):
        for chunk in range(lane_groups // 2):
            if with_lagged:
                lagged(chunk, lax.rem(step + 1, 2))
            if with_cross:
                cross(chunk * 2, lax.rem(step, 2))
                cross(chunk * 2 + 1, lax.rem(step, 2))

    @pl.when(step == 0)
    def _():
        table_copy.start()
        run(True, False)
        table_copy.wait()

    @pl.when(jnp.logical_and(step > 0, step < last))
    def _():
        run(True, True)

    @pl.when(step == last)
    def _():
        run(False, True)


def correlate(win, a, b, table):
    _, lane_groups, windows, tiles = a.shape[:4]
    channels = b.shape[3] * GROUP
    bins = lane_groups * LANES
    lags = table.shape[1]
    scaling = 1.0 / math.sqrt(windows * bins)
    whole = lambda x: pl.BlockSpec(x.shape, lambda t: (0,) * len(x.shape))
    return pl.pallas_call(
        functools.partial(correlate_kernel, scaling),
        grid=(tiles + 1,),
        in_specs=[pl.BlockSpec(memory_space=pltpu.SMEM)]
        + [whole(x) for x in (a, b)]
        + [pl.BlockSpec(memory_space=pltpu.HBM)],
        out_specs=pl.BlockSpec(
            (GROUP, 1, channels, lags), lambda t: (0, jnp.maximum(t - 1, 0), 0, 0)
        ),
        out_shape=jax.ShapeDtypeStruct((GROUP, tiles, channels, lags), jnp.bfloat16),
        scratch_shapes=[
            pltpu.VMEM((2, GROUP * channels, 2 * bins), jnp.bfloat16),
            pltpu.VMEM(table.shape, table.dtype),
            pltpu.SemaphoreType.DMA,
        ],
        compiler_params=pltpu.CompilerParams(vmem_limit_bytes=48 * 2**20),
        name="correlate",
    )(win, a, b, table)


def lag_rows_table(bin_total):
    bin_index = jnp.arange(bin_total, dtype=jnp.int32) + F0
    lag_index = jnp.arange(LAGS, dtype=jnp.int32) - LAGS // 2
    wrapped = bin_index[:, None] * lag_index[None, :] % NS
    phases = wrapped.astype(jnp.float32) * (2.0 * math.pi / NS)
    return jnp.concatenate([jnp.cos(phases), -jnp.sin(phases)], axis=0).astype(jnp.bfloat16)


def local(spectra, send_blocks, tile_slots):
    windows, owners = lax.axis_size("win"), lax.axis_size("pair")
    blocks, _, parts, channels, bins = spectra.shape
    tiles = tile_slots.shape[0]
    groups = channels // GROUP
    exchange = lambda x: lax.all_to_all(x, "pair", split_axis=0, concat_axis=0, tiled=True)
    pieces = (parts, bins // LANES, groups, tiles, GROUP, LANES)

    win = lax.axis_index("win").astype(jnp.int32).reshape(1)
    outgoing = whiten_spread(win, spectra, send_blocks[0].T, tile_slots.T)
    spread = exchange(outgoing.reshape(owners, blocks + 1, GROUP, LANES))
    spread, table = lax.optimization_barrier((spread, lag_rows_table(bins)))
    second, index = pick_second(spread, tiles)
    first = pick_first(index, spread, tiles)
    turn = [
        (w * owners + j, (w + j) % windows * owners + j)
        for w in range(windows)
        for j in range(owners)
    ]
    first = lax.ppermute(first, ("win", "pair"), turn)
    second = exchange(second)
    second, first = lax.optimization_barrier((second, first))
    b = lax.all_gather(second, "win", axis=0, tiled=False).reshape((windows,) + pieces)
    a = exchange(first).reshape(pieces)
    return correlate(win, a, b, table)


def solution(mesh):
    in_specs = (P("pair", "win", None, None, None), P("pair", None, None), P("pair", None))
    out_specs = P("win", "pair", None, None)
    return jax.shard_map(local, mesh=mesh, in_specs=in_specs, out_specs=out_specs, check_vma=False)
```

```python
import functools
import math

import jax
import jax.numpy as jnp
from jax import lax
from jax.experimental import pallas as pl
from jax.experimental.pallas import tpu as pltpu
from jax.sharding import PartitionSpec as P

LAGS = 1024
NS = 4096
F0 = 64
BAND = 64
LANES = 128
GROUP = 8
HALF = 64
SETTLE_FLOPS = 15 * 10**9


def whiten_kernel(win_ref, x_ref, sent_ref, slots_ref, out_ref, table_ref):
    blocks = x_ref.shape[0]
    _, lane_groups, groups = out_ref.shape[:3]
    step = pl.program_id(0)
    row_band = lax.broadcasted_iota(jnp.int32, (LANES, LANES), 0) // BAND
    column_band = lax.broadcasted_iota(jnp.int32, (LANES, LANES), 1) // BAND
    ones = jnp.where(row_band == column_band, 1.0, 0.0).astype(jnp.bfloat16)
    ones = jnp.concatenate([ones, ones, ones], axis=0)
    for lane_group in range(lane_groups):
        lanes = slice(lane_group * LANES, (lane_group + 1) * LANES)
        real = x_ref[:, 0, 0, :, lanes].astype(jnp.float32).reshape(blocks * 16, LANES)
        imag = x_ref[:, 0, 1, :, lanes].astype(jnp.float32).reshape(blocks * 16, LANES)
        rest = real * real + imag * imag
        terms = []
        for _ in range(3):
            terms.append(rest.astype(jnp.bfloat16))
            rest = rest - terms[-1].astype(jnp.float32)
        power = jnp.dot(jnp.concatenate(terms, axis=1), ones, preferred_element_type=jnp.float32)
        scale = lax.rsqrt(power * (1.0 / (2 * BAND)) + 1e-06)
        for part, rows in enumerate((real * scale, imag * scale)):
            rows = rows.reshape(blocks, 2, GROUP, LANES)
            for half in range(2):
                place = lax.rem(2 * step + half + groups - win_ref[0], groups)
                out_ref[part, lane_group, place, :blocks] = rows[:, half].astype(jnp.bfloat16)

    @pl.when(step == 0)
    def _():
        table_ref[...] = jnp.zeros_like(table_ref)
        table_ref[0:2, : sent_ref.shape[1]] = sent_ref[...].astype(jnp.float32)
        table_ref[2:4, : slots_ref.shape[1]] = slots_ref[...].astype(jnp.float32)
        piece = table_ref[...].astype(jnp.bfloat16)
        shape = out_ref.shape
        out_ref[:, :, :, blocks] = jnp.broadcast_to(piece, shape[:3] + shape[4:])


def whiten_spread(win, spectra, sent, slots):
    blocks, _, parts, channels, bins = spectra.shape
    shape = (parts, bins // LANES, channels // GROUP, blocks + 1, GROUP, LANES)
    return pl.pallas_call(
        whiten_kernel,
        grid=(channels // 16,),
        in_specs=[
            pl.BlockSpec(memory_space=pltpu.SMEM),
            pl.BlockSpec((blocks, 1, parts, 16, bins), lambda g: (0, 0, 0, g, 0)),
            pl.BlockSpec(sent.shape, lambda g: (0, 0)),
            pl.BlockSpec(slots.shape, lambda g: (0, 0)),
        ],
        out_specs=pl.BlockSpec(shape, lambda g: (0,) * len(shape)),
        out_shape=jax.ShapeDtypeStruct(shape, jnp.bfloat16),
        scratch_shapes=[pltpu.VMEM((GROUP, LANES), jnp.float32)],
        compiler_params=pltpu.CompilerParams(vmem_limit_bytes=60 * 2**20),
        name="whiten_spread",
    )(win, spectra, sent, slots)


def copy_pieces(place_ref, x_ref, out_ref, start):
    flat = x_ref.reshape((x_ref.shape[0] * x_ref.shape[1],) + x_ref.shape[2:])

    def one_owner(owner, carry):
        for tile in range(out_ref.shape[1]):
            out_ref[owner, tile] = flat[place_ref[owner, start + tile]]
        return carry

    lax.fori_loop(0, out_ref.shape[0], one_owner, 0, unroll=4)


def pick_second_kernel(x_ref, out_ref, index_ref, table_ref, place_ref, sem):
    owners, stride = x_ref.shape[:2]
    tiles = out_ref.shape[1]
    table_ref[...] = x_ref[:, stride - 1].astype(jnp.float32).reshape(table_ref.shape)
    sent = [table_ref[pl.ds(k, owners, stride=GROUP), :] for k in range(2)]
    lane = lax.broadcasted_iota(jnp.int32, (owners, LANES), 1)
    by_owner = jnp.concatenate(sent, axis=0).T[:owners].astype(jnp.int32)
    by_owner = by_owner + stride * (lane % HALF)
    places = jnp.zeros((owners, LANES), jnp.int32)
    for part in range(2):
        slots = table_ref[pl.ds(2 + part, owners, stride=GROUP), :].astype(jnp.int32)
        for tile in range(tiles):
            slot = slots[:, tile : tile + 1]
            hit = lane == (slot % 2) * HALF + slot // 2
            place = jnp.sum(jnp.where(hit, by_owner, 0), axis=1, keepdims=True)
            places = jnp.where(lane == part * tiles + tile, place, places)
    index_ref[...] = places
    copy = pltpu.make_async_copy(index_ref, place_ref, sem)
    copy.start()
    copy.wait()
    copy_pieces(place_ref, x_ref, out_ref, tiles)


def pick_second(spread, tiles):
    owners = spread.shape[0]
    return pl.pallas_call(
        pick_second_kernel,
        in_specs=[pl.BlockSpec(memory_space=pltpu.VMEM)],
        out_specs=[pl.BlockSpec(memory_space=pltpu.VMEM)] * 2,
        out_shape=[
            jax.ShapeDtypeStruct((owners, tiles, GROUP, LANES), jnp.bfloat16),
            jax.ShapeDtypeStruct((owners, LANES), jnp.int32),
        ],
        scratch_shapes=[
            pltpu.VMEM((owners * GROUP, LANES), jnp.float32),
            pltpu.SMEM((owners, LANES), jnp.int32),
            pltpu.SemaphoreType.DMA,
        ],
        compiler_params=pltpu.CompilerParams(vmem_limit_bytes=24 * 2**20),
        name="pick_second",
    )(spread)


def pick_first(index, spread, tiles):
    owners = spread.shape[0]
    return pl.pallas_call(
        lambda place_ref, x_ref, out_ref: copy_pieces(place_ref, x_ref, out_ref, 0),
        in_specs=[
            pl.BlockSpec(memory_space=pltpu.SMEM),
            pl.BlockSpec(memory_space=pltpu.VMEM),
        ],
        out_specs=pl.BlockSpec(memory_space=pltpu.VMEM),
        out_shape=jax.ShapeDtypeStruct((owners, tiles, GROUP, LANES), jnp.bfloat16),
        compiler_params=pltpu.CompilerParams(vmem_limit_bytes=24 * 2**20),
        name="pick_first",
    )(index, spread)


def correlate_kernel(scaling, win_ref, a_ref, *refs):
    windows = a_ref.shape[2]
    b_refs, table_hbm = refs[:windows], refs[windows]
    out_ref, stack_ref, table_ref, sem = refs[windows + 1 :]
    step = pl.program_id(0)
    last = pl.num_programs(0) - 1
    _, lane_groups, groups = b_refs[0].shape[:3]
    bins = lane_groups * LANES
    channels = groups * GROUP
    places = [
        [lax.rem(group + distance + groups - win_ref[0], groups) for group in range(groups)]
        for distance in range(windows)
    ]
    table_copy = pltpu.make_async_copy(table_hbm, table_ref, sem)

    def cross(lane_group, slot):
        lanes = lane_group * LANES
        a = [
            [a_ref[part, lane_group, w, step].astype(jnp.float32) for part in range(2)]
            for w in range(windows)
        ]
        for pair in range(groups // 2):
            b = [
                [
                    [
                        b_refs[w][part, lane_group, places[w][pair * 2 + half], step].astype(
                            jnp.float32
                        )
                        for part in range(2)
                    ]
                    for w in range(windows)
                ]
                for half in range(2)
            ]
            for i in range(GROUP):
                rows = [[None, None], [None, None]]
                for w in range(windows):
                    a0 = jnp.broadcast_to(a[w][0][i : i + 1], (GROUP, LANES))
                    a1 = jnp.broadcast_to(a[w][1][i : i + 1], (GROUP, LANES))
                    for half in range(2):
                        b0, b1 = b[half][w]
                        real = a0 * b0 + a1 * b1
                        imag = a1 * b0 - a0 * b1
                        if w:
                            real += rows[half][0]
                            imag += rows[half][1]
                        rows[half] = [real, imag]
                start = i * channels + pair * 2 * GROUP
                for part in range(2):
                    joined = jnp.concatenate([rows[0][part], rows[1][part]], axis=0)
                    stack_ref[
                        slot, start : start + 2 * GROUP, pl.ds(part * bins + lanes, LANES)
                    ] = joined.astype(jnp.bfloat16)

    def lagged(chunk, slot):
        columns = pl.ds(chunk * 2 * LANES, 2 * LANES)
        rows = jnp.dot(stack_ref[slot], table_ref[:, columns], preferred_element_type=jnp.float32)
        rows = (rows * scaling).astype(jnp.bfloat16)
        out_ref[:, 0, :, columns] = rows.reshape(GROUP, channels, 2 * LANES)

    def run(with_cross, with_lagged):
        for chunk in range(lane_groups // 2):
            if with_lagged:
                lagged(chunk, lax.rem(step + 1, 2))
            if with_cross:
                cross(chunk * 2, lax.rem(step, 2))
                cross(chunk * 2 + 1, lax.rem(step, 2))

    @pl.when(step == 0)
    def _():
        table_copy.start()
        run(True, False)
        table_copy.wait()

    @pl.when(jnp.logical_and(step > 0, step < last))
    def _():
        run(True, True)

    @pl.when(step == last)
    def _():
        run(False, True)


def correlate(win, a, b, table):
    _, lane_groups, windows, tiles = a.shape[:4]
    channels = b[0].shape[2] * GROUP
    bins = lane_groups * LANES
    lags = table.shape[1]
    scaling = 1.0 / math.sqrt(windows * bins)
    whole = lambda x: pl.BlockSpec(x.shape, lambda t: (0,) * len(x.shape))
    return pl.pallas_call(
        functools.partial(correlate_kernel, scaling),
        grid=(tiles + 1,),
        in_specs=[pl.BlockSpec(memory_space=pltpu.SMEM)]
        + [whole(x) for x in (a, *b)]
        + [pl.BlockSpec(memory_space=pltpu.HBM)],
        out_specs=pl.BlockSpec(
            (GROUP, 1, channels, lags), lambda t: (0, jnp.maximum(t - 1, 0), 0, 0)
        ),
        out_shape=jax.ShapeDtypeStruct((GROUP, tiles, channels, lags), jnp.bfloat16),
        scratch_shapes=[
            pltpu.VMEM((2, GROUP * channels, 2 * bins), jnp.bfloat16),
            pltpu.VMEM(table.shape, table.dtype),
            pltpu.SemaphoreType.DMA,
        ],
        compiler_params=pltpu.CompilerParams(vmem_limit_bytes=48 * 2**20),
        name="correlate",
    )(win, a, *b, table)


def settle_kernel(win_ref, *refs):
    refs[-1][0] = win_ref[0]


def settle(win, arrays):
    return pl.pallas_call(
        settle_kernel,
        in_specs=[pl.BlockSpec(memory_space=pltpu.SMEM)]
        + [pl.BlockSpec(memory_space=pl.ANY)] * len(arrays),
        out_specs=pl.BlockSpec(memory_space=pltpu.SMEM),
        out_shape=jax.ShapeDtypeStruct(win.shape, win.dtype),
        compiler_params=pltpu.CompilerParams(vmem_limit_bytes=2**20),
        cost_estimate=pl.CostEstimate(flops=SETTLE_FLOPS, bytes_accessed=0, transcendentals=0),
        name="settle",
    )(win, *arrays)


def lag_rows_table(bin_total):
    bin_index = jnp.arange(bin_total, dtype=jnp.int32) + F0
    lag_index = jnp.arange(LAGS, dtype=jnp.int32) - LAGS // 2
    wrapped = bin_index[:, None] * lag_index[None, :] % NS
    phases = wrapped.astype(jnp.float32) * (2.0 * math.pi / NS)
    return jnp.concatenate([jnp.cos(phases), -jnp.sin(phases)], axis=0).astype(jnp.bfloat16)


def local(spectra, send_blocks, tile_slots):
    windows, owners = lax.axis_size("win"), lax.axis_size("pair")
    blocks, _, parts, channels, bins = spectra.shape
    tiles = tile_slots.shape[0]
    groups = channels // GROUP
    exchange = lambda x: lax.all_to_all(x, "pair", split_axis=0, concat_axis=0, tiled=True)
    pieces = (parts, bins // LANES, groups, tiles, GROUP, LANES)

    win = lax.axis_index("win").astype(jnp.int32).reshape(1)
    outgoing = whiten_spread(win, spectra, send_blocks[0].T, tile_slots.T)
    spread = exchange(outgoing.reshape(owners, blocks + 1, GROUP, LANES))
    spread, table = lax.optimization_barrier((spread, lag_rows_table(bins)))
    second, index = pick_second(spread, tiles)
    first = pick_first(index, spread, tiles)
    turn = [
        (w * owners + j, (w + j) % windows * owners + j)
        for w in range(windows)
        for j in range(owners)
    ]
    first = lax.ppermute(first, ("win", "pair"), turn)
    second = exchange(second)
    second, first = lax.optimization_barrier((second, first))
    b = [second]
    for distance in range(1, windows):
        step = [(w, (w + distance) % windows) for w in range(windows)]
        b.append(lax.ppermute(second, "win", step))
    win = settle(win, b[1:])
    a = exchange(first).reshape(pieces)
    return correlate(win, a, [x.reshape(pieces) for x in b], table)


def solution(mesh):
    in_specs = (P("pair", "win", None, None, None), P("pair", None, None), P("pair", None))
    out_specs = P("win", "pair", None, None)
    return jax.shard_map(local, mesh=mesh, in_specs=in_specs, out_specs=out_specs, check_vma=False)
```

```python
import functools
import math

import jax
import jax.numpy as jnp
from jax import lax
from jax.experimental import pallas as pl
from jax.experimental.pallas import tpu as pltpu
from jax.sharding import PartitionSpec as P

LAGS = 1024
NS = 4096
F0 = 64
BAND = 64
LANES = 128
GROUP = 8
HALF = 64
SETTLE_FLOPS = 8 * 10**9


def whiten_kernel(win_ref, x_ref, sent_ref, slots_ref, out_ref, table_ref):
    blocks = x_ref.shape[0]
    _, lane_groups, groups = out_ref.shape[:3]
    step = pl.program_id(0)
    row_band = lax.broadcasted_iota(jnp.int32, (LANES, LANES), 0) // BAND
    column_band = lax.broadcasted_iota(jnp.int32, (LANES, LANES), 1) // BAND
    ones = jnp.where(row_band == column_band, 1.0, 0.0).astype(jnp.bfloat16)
    ones = jnp.concatenate([ones, ones, ones], axis=0)
    for lane_group in range(lane_groups):
        lanes = slice(lane_group * LANES, (lane_group + 1) * LANES)
        real = x_ref[:, 0, 0, :, lanes].astype(jnp.float32).reshape(blocks * 16, LANES)
        imag = x_ref[:, 0, 1, :, lanes].astype(jnp.float32).reshape(blocks * 16, LANES)
        rest = real * real + imag * imag
        terms = []
        for _ in range(3):
            terms.append(rest.astype(jnp.bfloat16))
            rest = rest - terms[-1].astype(jnp.float32)
        power = jnp.dot(jnp.concatenate(terms, axis=1), ones, preferred_element_type=jnp.float32)
        scale = lax.rsqrt(power * (1.0 / (2 * BAND)) + 1e-06)
        for part, rows in enumerate((real * scale, imag * scale)):
            rows = rows.reshape(blocks, 2, GROUP, LANES)
            for half in range(2):
                place = lax.rem(2 * step + half + groups - win_ref[0], groups)
                out_ref[part, lane_group, place, :blocks] = rows[:, half].astype(jnp.bfloat16)

    @pl.when(step == 0)
    def _():
        table_ref[...] = jnp.zeros_like(table_ref)
        table_ref[0:2, : sent_ref.shape[1]] = sent_ref[...].astype(jnp.float32)
        table_ref[2:4, : slots_ref.shape[1]] = slots_ref[...].astype(jnp.float32)
        piece = table_ref[...].astype(jnp.bfloat16)
        shape = out_ref.shape
        out_ref[:, :, :, blocks] = jnp.broadcast_to(piece, shape[:3] + shape[4:])


def whiten_spread(win, spectra, sent, slots):
    blocks, _, parts, channels, bins = spectra.shape
    shape = (parts, bins // LANES, channels // GROUP, blocks + 1, GROUP, LANES)
    return pl.pallas_call(
        whiten_kernel,
        grid=(channels // 16,),
        in_specs=[
            pl.BlockSpec(memory_space=pltpu.SMEM),
            pl.BlockSpec((blocks, 1, parts, 16, bins), lambda g: (0, 0, 0, g, 0)),
            pl.BlockSpec(sent.shape, lambda g: (0, 0)),
            pl.BlockSpec(slots.shape, lambda g: (0, 0)),
        ],
        out_specs=pl.BlockSpec(shape, lambda g: (0,) * len(shape)),
        out_shape=jax.ShapeDtypeStruct(shape, jnp.bfloat16),
        scratch_shapes=[pltpu.VMEM((GROUP, LANES), jnp.float32)],
        compiler_params=pltpu.CompilerParams(vmem_limit_bytes=60 * 2**20),
        name="whiten_spread",
    )(win, spectra, sent, slots)


def copy_pieces(place_ref, x_ref, out_ref, start):
    flat = x_ref.reshape((x_ref.shape[0] * x_ref.shape[1],) + x_ref.shape[2:])

    def one_owner(owner, carry):
        for tile in range(out_ref.shape[1]):
            out_ref[owner, tile] = flat[place_ref[owner, start + tile]]
        return carry

    lax.fori_loop(0, out_ref.shape[0], one_owner, 0, unroll=4)


def pick_second_kernel(x_ref, out_ref, index_ref, table_ref, place_ref, sem):
    owners, stride = x_ref.shape[:2]
    tiles = out_ref.shape[1]
    table_ref[...] = x_ref[:, stride - 1].astype(jnp.float32).reshape(table_ref.shape)
    sent = [table_ref[pl.ds(k, owners, stride=GROUP), :] for k in range(2)]
    lane = lax.broadcasted_iota(jnp.int32, (owners, LANES), 1)
    by_owner = jnp.concatenate(sent, axis=0).T[:owners].astype(jnp.int32)
    by_owner = by_owner + stride * (lane % HALF)
    places = jnp.zeros((owners, LANES), jnp.int32)
    for part in range(2):
        slots = table_ref[pl.ds(2 + part, owners, stride=GROUP), :].astype(jnp.int32)
        for tile in range(tiles):
            slot = slots[:, tile : tile + 1]
            hit = lane == (slot % 2) * HALF + slot // 2
            place = jnp.sum(jnp.where(hit, by_owner, 0), axis=1, keepdims=True)
            places = jnp.where(lane == part * tiles + tile, place, places)
    index_ref[...] = places
    copy = pltpu.make_async_copy(index_ref, place_ref, sem)
    copy.start()
    copy.wait()
    copy_pieces(place_ref, x_ref, out_ref, tiles)


def pick_second(spread, tiles):
    owners = spread.shape[0]
    return pl.pallas_call(
        pick_second_kernel,
        in_specs=[pl.BlockSpec(memory_space=pltpu.VMEM)],
        out_specs=[pl.BlockSpec(memory_space=pltpu.VMEM)] * 2,
        out_shape=[
            jax.ShapeDtypeStruct((owners, tiles, GROUP, LANES), jnp.bfloat16),
            jax.ShapeDtypeStruct((owners, LANES), jnp.int32),
        ],
        scratch_shapes=[
            pltpu.VMEM((owners * GROUP, LANES), jnp.float32),
            pltpu.SMEM((owners, LANES), jnp.int32),
            pltpu.SemaphoreType.DMA,
        ],
        compiler_params=pltpu.CompilerParams(vmem_limit_bytes=24 * 2**20),
        name="pick_second",
    )(spread)


def pick_first(index, spread, tiles):
    owners = spread.shape[0]
    return pl.pallas_call(
        lambda place_ref, x_ref, out_ref: copy_pieces(place_ref, x_ref, out_ref, 0),
        in_specs=[
            pl.BlockSpec(memory_space=pltpu.SMEM),
            pl.BlockSpec(memory_space=pltpu.VMEM),
        ],
        out_specs=pl.BlockSpec(memory_space=pltpu.VMEM),
        out_shape=jax.ShapeDtypeStruct((owners, tiles, GROUP, LANES), jnp.bfloat16),
        compiler_params=pltpu.CompilerParams(vmem_limit_bytes=24 * 2**20),
        name="pick_first",
    )(index, spread)


def correlate_kernel(scaling, win_ref, a_ref, *refs):
    windows = a_ref.shape[2]
    b_refs, table_hbm = refs[:windows], refs[windows]
    out_ref, stack_ref, table_ref, sem = refs[windows + 1 :]
    step = pl.program_id(0)
    last = pl.num_programs(0) - 1
    _, lane_groups, groups = b_refs[0].shape[:3]
    bins = lane_groups * LANES
    channels = groups * GROUP
    places = [
        [lax.rem(group + distance + groups - win_ref[0], groups) for group in range(groups)]
        for distance in range(windows)
    ]
    table_copy = pltpu.make_async_copy(table_hbm, table_ref, sem)

    def cross(lane_group, slot):
        lanes = lane_group * LANES
        a = [
            [a_ref[part, lane_group, w, step].astype(jnp.float32) for part in range(2)]
            for w in range(windows)
        ]
        for pair in range(groups // 2):
            b = [
                [
                    [
                        b_refs[w][part, lane_group, places[w][pair * 2 + half], step].astype(
                            jnp.float32
                        )
                        for part in range(2)
                    ]
                    for w in range(windows)
                ]
                for half in range(2)
            ]
            for i in range(GROUP):
                rows = [[None, None], [None, None]]
                for w in range(windows):
                    a0 = jnp.broadcast_to(a[w][0][i : i + 1], (GROUP, LANES))
                    a1 = jnp.broadcast_to(a[w][1][i : i + 1], (GROUP, LANES))
                    for half in range(2):
                        b0, b1 = b[half][w]
                        real = a0 * b0 + a1 * b1
                        imag = a1 * b0 - a0 * b1
                        if w:
                            real += rows[half][0]
                            imag += rows[half][1]
                        rows[half] = [real, imag]
                start = i * channels + pair * 2 * GROUP
                for part in range(2):
                    joined = jnp.concatenate([rows[0][part], rows[1][part]], axis=0)
                    stack_ref[
                        slot, start : start + 2 * GROUP, pl.ds(part * bins + lanes, LANES)
                    ] = joined.astype(jnp.bfloat16)

    def lagged(chunk, slot):
        columns = pl.ds(chunk * 2 * LANES, 2 * LANES)
        rows = jnp.dot(stack_ref[slot], table_ref[:, columns], preferred_element_type=jnp.float32)
        rows = (rows * scaling).astype(jnp.bfloat16)
        out_ref[:, 0, :, columns] = rows.reshape(GROUP, channels, 2 * LANES)

    def run(with_cross, with_lagged):
        for chunk in range(lane_groups // 2):
            if with_lagged:
                lagged(chunk, lax.rem(step + 1, 2))
            if with_cross:
                cross(chunk * 2, lax.rem(step, 2))
                cross(chunk * 2 + 1, lax.rem(step, 2))

    @pl.when(step == 0)
    def _():
        table_copy.start()
        run(True, False)
        table_copy.wait()

    @pl.when(jnp.logical_and(step > 0, step < last))
    def _():
        run(True, True)

    @pl.when(step == last)
    def _():
        run(False, True)


def correlate(win, a, b, table):
    _, lane_groups, windows, tiles = a.shape[:4]
    channels = b[0].shape[2] * GROUP
    bins = lane_groups * LANES
    lags = table.shape[1]
    scaling = 1.0 / math.sqrt(windows * bins)
    whole = lambda x: pl.BlockSpec(x.shape, lambda t: (0,) * len(x.shape))
    return pl.pallas_call(
        functools.partial(correlate_kernel, scaling),
        grid=(tiles + 1,),
        in_specs=[pl.BlockSpec(memory_space=pltpu.SMEM)]
        + [whole(x) for x in (a, *b)]
        + [pl.BlockSpec(memory_space=pltpu.HBM)],
        out_specs=pl.BlockSpec(
            (GROUP, 1, channels, lags), lambda t: (0, jnp.maximum(t - 1, 0), 0, 0)
        ),
        out_shape=jax.ShapeDtypeStruct((GROUP, tiles, channels, lags), jnp.bfloat16),
        scratch_shapes=[
            pltpu.VMEM((2, GROUP * channels, 2 * bins), jnp.bfloat16),
            pltpu.VMEM(table.shape, table.dtype),
            pltpu.SemaphoreType.DMA,
        ],
        compiler_params=pltpu.CompilerParams(vmem_limit_bytes=48 * 2**20),
        name="correlate",
    )(win, a, *b, table)


def settle_kernel(win_ref, *refs):
    refs[-1][0] = win_ref[0]


def settle(win, arrays):
    return pl.pallas_call(
        settle_kernel,
        in_specs=[pl.BlockSpec(memory_space=pltpu.SMEM)]
        + [pl.BlockSpec(memory_space=pl.ANY)] * len(arrays),
        out_specs=pl.BlockSpec(memory_space=pltpu.SMEM),
        out_shape=jax.ShapeDtypeStruct(win.shape, win.dtype),
        compiler_params=pltpu.CompilerParams(vmem_limit_bytes=2**20),
        cost_estimate=pl.CostEstimate(flops=SETTLE_FLOPS, bytes_accessed=0, transcendentals=0),
        name="settle",
    )(win, *arrays)


def lag_rows_table(bin_total):
    bin_index = jnp.arange(bin_total, dtype=jnp.int32) + F0
    lag_index = jnp.arange(LAGS, dtype=jnp.int32) - LAGS // 2
    wrapped = bin_index[:, None] * lag_index[None, :] % NS
    phases = wrapped.astype(jnp.float32) * (2.0 * math.pi / NS)
    return jnp.concatenate([jnp.cos(phases), -jnp.sin(phases)], axis=0).astype(jnp.bfloat16)


def local(spectra, send_blocks, tile_slots):
    windows, owners = lax.axis_size("win"), lax.axis_size("pair")
    blocks, _, parts, channels, bins = spectra.shape
    tiles = tile_slots.shape[0]
    groups = channels // GROUP
    exchange = lambda x: lax.all_to_all(x, "pair", split_axis=0, concat_axis=0, tiled=True)
    pieces = (parts, bins // LANES, groups, tiles, GROUP, LANES)

    win = lax.axis_index("win").astype(jnp.int32).reshape(1)
    outgoing = whiten_spread(win, spectra, send_blocks[0].T, tile_slots.T)
    spread = exchange(outgoing.reshape(owners, blocks + 1, GROUP, LANES))
    spread, table = lax.optimization_barrier((spread, lag_rows_table(bins)))
    second, index = pick_second(spread, tiles)
    first = pick_first(index, spread, tiles)
    turn = [
        (w * owners + j, (w + j) % windows * owners + j)
        for w in range(windows)
        for j in range(owners)
    ]
    first = lax.ppermute(first, ("win", "pair"), turn)
    second = exchange(second)
    second, first = lax.optimization_barrier((second, first))
    b = [second]
    for distance in range(1, windows):
        step = [(w, (w + distance) % windows) for w in range(windows)]
        b.append(lax.ppermute(second, "win", step))
    win = settle(win, b[windows // 2 : windows // 2 + 1])
    a = exchange(first).reshape(pieces)
    return correlate(win, a, [x.reshape(pieces) for x in b], table)


def solution(mesh):
    in_specs = (P("pair", "win", None, None, None), P("pair", None, None), P("pair", None))
    out_specs = P("win", "pair", None, None)
    return jax.shard_map(local, mesh=mesh, in_specs=in_specs, out_specs=out_specs, check_vma=False)
```

```python
import functools
import math

import jax
import jax.numpy as jnp
from jax import lax
from jax.experimental import pallas as pl
from jax.experimental.pallas import tpu as pltpu
from jax.sharding import PartitionSpec as P

LAGS = 1024
NS = 4096
F0 = 64
BAND = 64
LANES = 128
GROUP = 8
HALF = 64
SETTLE_FLOPS = 8 * 10**9


def whiten_kernel(win_ref, x_ref, sent_ref, slots_ref, out_ref, table_ref):
    blocks = x_ref.shape[0]
    _, lane_groups, groups = out_ref.shape[:3]
    step = pl.program_id(0)
    row_band = lax.broadcasted_iota(jnp.int32, (LANES, LANES), 0) // BAND
    column_band = lax.broadcasted_iota(jnp.int32, (LANES, LANES), 1) // BAND
    ones = jnp.where(row_band == column_band, 1.0, 0.0).astype(jnp.bfloat16)
    ones = jnp.concatenate([ones, ones, ones], axis=0)
    for lane_group in range(lane_groups):
        lanes = slice(lane_group * LANES, (lane_group + 1) * LANES)
        real = x_ref[:, 0, 0, :, lanes].astype(jnp.float32).reshape(blocks * 16, LANES)
        imag = x_ref[:, 0, 1, :, lanes].astype(jnp.float32).reshape(blocks * 16, LANES)
        rest = real * real + imag * imag
        terms = []
        for _ in range(3):
            terms.append(rest.astype(jnp.bfloat16))
            rest = rest - terms[-1].astype(jnp.float32)
        power = jnp.dot(jnp.concatenate(terms, axis=1), ones, preferred_element_type=jnp.float32)
        scale = lax.rsqrt(power * (1.0 / (2 * BAND)) + 1e-06)
        for part, rows in enumerate((real * scale, imag * scale)):
            rows = rows.reshape(blocks, 2, GROUP, LANES)
            for half in range(2):
                place = lax.rem(2 * step + half + groups - win_ref[0], groups)
                out_ref[part, lane_group, place, :blocks] = rows[:, half].astype(jnp.bfloat16)

    @pl.when(step == 0)
    def _():
        table_ref[...] = jnp.zeros_like(table_ref)
        table_ref[0:2, : sent_ref.shape[1]] = sent_ref[...].astype(jnp.float32)
        table_ref[2:4, : slots_ref.shape[1]] = slots_ref[...].astype(jnp.float32)
        piece = table_ref[...].astype(jnp.bfloat16)
        shape = out_ref.shape
        out_ref[:, :, :, blocks] = jnp.broadcast_to(piece, shape[:3] + shape[4:])


def whiten_spread(win, spectra, sent, slots):
    blocks, _, parts, channels, bins = spectra.shape
    shape = (parts, bins // LANES, channels // GROUP, blocks + 1, GROUP, LANES)
    return pl.pallas_call(
        whiten_kernel,
        grid=(channels // 16,),
        in_specs=[
            pl.BlockSpec(memory_space=pltpu.SMEM),
            pl.BlockSpec((blocks, 1, parts, 16, bins), lambda g: (0, 0, 0, g, 0)),
            pl.BlockSpec(sent.shape, lambda g: (0, 0)),
            pl.BlockSpec(slots.shape, lambda g: (0, 0)),
        ],
        out_specs=pl.BlockSpec(shape, lambda g: (0,) * len(shape)),
        out_shape=jax.ShapeDtypeStruct(shape, jnp.bfloat16),
        scratch_shapes=[pltpu.VMEM((GROUP, LANES), jnp.float32)],
        compiler_params=pltpu.CompilerParams(vmem_limit_bytes=60 * 2**20),
        name="whiten_spread",
    )(win, spectra, sent, slots)


def copy_pieces(place_ref, x_ref, out_ref, start):
    flat = x_ref.reshape((x_ref.shape[0] * x_ref.shape[1],) + x_ref.shape[2:])

    def one_owner(owner, carry):
        for tile in range(out_ref.shape[1]):
            out_ref[owner, tile] = flat[place_ref[owner, start + tile]]
        return carry

    lax.fori_loop(0, out_ref.shape[0], one_owner, 0, unroll=4)


def pick_second_kernel(x_ref, out_ref, index_ref, table_ref, place_ref, sem):
    owners, stride = x_ref.shape[:2]
    tiles = out_ref.shape[1]
    table_ref[...] = x_ref[:, stride - 1].astype(jnp.float32).reshape(table_ref.shape)
    sent = [table_ref[pl.ds(k, owners, stride=GROUP), :] for k in range(2)]
    lane = lax.broadcasted_iota(jnp.int32, (owners, LANES), 1)
    by_owner = jnp.concatenate(sent, axis=0).T[:owners].astype(jnp.int32)
    by_owner = by_owner + stride * (lane % HALF)
    places = jnp.zeros((owners, LANES), jnp.int32)
    for part in range(2):
        slots = table_ref[pl.ds(2 + part, owners, stride=GROUP), :].astype(jnp.int32)
        for tile in range(tiles):
            slot = slots[:, tile : tile + 1]
            hit = lane == (slot % 2) * HALF + slot // 2
            place = jnp.sum(jnp.where(hit, by_owner, 0), axis=1, keepdims=True)
            places = jnp.where(lane == part * tiles + tile, place, places)
    index_ref[...] = places
    copy = pltpu.make_async_copy(index_ref, place_ref, sem)
    copy.start()
    copy.wait()
    copy_pieces(place_ref, x_ref, out_ref, tiles)


def pick_second(spread, tiles):
    owners = spread.shape[0]
    return pl.pallas_call(
        pick_second_kernel,
        in_specs=[pl.BlockSpec(memory_space=pltpu.VMEM)],
        out_specs=[pl.BlockSpec(memory_space=pltpu.VMEM)] * 2,
        out_shape=[
            jax.ShapeDtypeStruct((owners, tiles, GROUP, LANES), jnp.bfloat16),
            jax.ShapeDtypeStruct((owners, LANES), jnp.int32),
        ],
        scratch_shapes=[
            pltpu.VMEM((owners * GROUP, LANES), jnp.float32),
            pltpu.SMEM((owners, LANES), jnp.int32),
            pltpu.SemaphoreType.DMA,
        ],
        compiler_params=pltpu.CompilerParams(vmem_limit_bytes=24 * 2**20),
        name="pick_second",
    )(spread)


def pick_first(index, spread, tiles):
    owners = spread.shape[0]
    return pl.pallas_call(
        lambda place_ref, x_ref, out_ref: copy_pieces(place_ref, x_ref, out_ref, 0),
        in_specs=[
            pl.BlockSpec(memory_space=pltpu.SMEM),
            pl.BlockSpec(memory_space=pltpu.VMEM),
        ],
        out_specs=pl.BlockSpec(memory_space=pltpu.VMEM),
        out_shape=jax.ShapeDtypeStruct((owners, tiles, GROUP, LANES), jnp.bfloat16),
        compiler_params=pltpu.CompilerParams(vmem_limit_bytes=24 * 2**20),
        name="pick_first",
    )(index, spread)


def correlate_kernel(scaling, win_ref, a_ref, *refs):
    windows = a_ref.shape[2]
    b_refs, table_hbm = refs[:windows], refs[windows]
    out_ref, stack_ref, table_ref, sem = refs[windows + 1 :]
    step = pl.program_id(0)
    last = pl.num_programs(0) - 1
    _, lane_groups, groups = b_refs[0].shape[:3]
    bins = lane_groups * LANES
    channels = groups * GROUP
    places = [
        [lax.rem(group + distance + groups - win_ref[0], groups) for group in range(groups)]
        for distance in range(windows)
    ]
    table_copy = pltpu.make_async_copy(table_hbm, table_ref, sem)

    def cross(lane_group, slot):
        lanes = lane_group * LANES
        a = [
            [a_ref[part, lane_group, w, step].astype(jnp.float32) for part in range(2)]
            for w in range(windows)
        ]
        for pair in range(groups // 2):
            b = [
                [
                    [
                        b_refs[w][part, lane_group, places[w][pair * 2 + half], step].astype(
                            jnp.float32
                        )
                        for part in range(2)
                    ]
                    for w in range(windows)
                ]
                for half in range(2)
            ]
            for i in range(GROUP):
                rows = [[None, None], [None, None]]
                for w in range(windows):
                    a0 = jnp.broadcast_to(a[w][0][i : i + 1], (GROUP, LANES))
                    a1 = jnp.broadcast_to(a[w][1][i : i + 1], (GROUP, LANES))
                    for half in range(2):
                        b0, b1 = b[half][w]
                        real = a0 * b0 + a1 * b1
                        imag = a1 * b0 - a0 * b1
                        if w:
                            real += rows[half][0]
                            imag += rows[half][1]
                        rows[half] = [real, imag]
                start = i * channels + pair * 2 * GROUP
                for part in range(2):
                    joined = jnp.concatenate([rows[0][part], rows[1][part]], axis=0)
                    stack_ref[
                        slot, start : start + 2 * GROUP, pl.ds(part * bins + lanes, LANES)
                    ] = joined.astype(jnp.bfloat16)

    def lagged(chunk, slot):
        columns = pl.ds(chunk * 2 * LANES, 2 * LANES)
        rows = jnp.dot(stack_ref[slot], table_ref[:, columns], preferred_element_type=jnp.float32)
        rows = (rows * scaling).astype(jnp.bfloat16)
        out_ref[:, 0, :, columns] = rows.reshape(GROUP, channels, 2 * LANES)

    def run(with_cross, with_lagged):
        for chunk in range(lane_groups // 2):
            if with_lagged:
                lagged(chunk, lax.rem(step + 1, 2))
            if with_cross:
                cross(chunk * 2, lax.rem(step, 2))
                cross(chunk * 2 + 1, lax.rem(step, 2))

    @pl.when(step == 0)
    def _():
        table_copy.start()
        run(True, False)
        table_copy.wait()

    @pl.when(jnp.logical_and(step > 0, step < last))
    def _():
        run(True, True)

    @pl.when(step == last)
    def _():
        run(False, True)


def correlate(win, a, b, table):
    _, lane_groups, windows, tiles = a.shape[:4]
    channels = b[0].shape[2] * GROUP
    bins = lane_groups * LANES
    lags = table.shape[1]
    scaling = 1.0 / math.sqrt(windows * bins)
    whole = lambda x: pl.BlockSpec(x.shape, lambda t: (0,) * len(x.shape))
    return pl.pallas_call(
        functools.partial(correlate_kernel, scaling),
        grid=(tiles + 1,),
        in_specs=[pl.BlockSpec(memory_space=pltpu.SMEM)]
        + [whole(x) for x in (a, *b)]
        + [pl.BlockSpec(memory_space=pltpu.HBM)],
        out_specs=pl.BlockSpec(
            (GROUP, 1, channels, lags), lambda t: (0, jnp.maximum(t - 1, 0), 0, 0)
        ),
        out_shape=jax.ShapeDtypeStruct((GROUP, tiles, channels, lags), jnp.bfloat16),
        scratch_shapes=[
            pltpu.VMEM((2, GROUP * channels, 2 * bins), jnp.bfloat16),
            pltpu.VMEM(table.shape, table.dtype),
            pltpu.SemaphoreType.DMA,
        ],
        compiler_params=pltpu.CompilerParams(vmem_limit_bytes=48 * 2**20),
        name="correlate",
    )(win, a, *b, table)


def settle_kernel(win_ref, *refs):
    refs[-1][0] = win_ref[0]


def settle(win, arrays):
    return pl.pallas_call(
        settle_kernel,
        in_specs=[pl.BlockSpec(memory_space=pltpu.SMEM)]
        + [pl.BlockSpec(memory_space=pl.ANY)] * len(arrays),
        out_specs=pl.BlockSpec(memory_space=pltpu.SMEM),
        out_shape=jax.ShapeDtypeStruct(win.shape, win.dtype),
        compiler_params=pltpu.CompilerParams(vmem_limit_bytes=2**20),
        cost_estimate=pl.CostEstimate(flops=SETTLE_FLOPS, bytes_accessed=0, transcendentals=0),
        name="settle",
    )(win, *arrays)


def lag_rows_table(bin_total):
    bin_index = jnp.arange(bin_total, dtype=jnp.int32) + F0
    lag_index = jnp.arange(LAGS, dtype=jnp.int32) - LAGS // 2
    wrapped = bin_index[:, None] * lag_index[None, :] % NS
    phases = wrapped.astype(jnp.float32) * (2.0 * math.pi / NS)
    return jnp.concatenate([jnp.cos(phases), -jnp.sin(phases)], axis=0).astype(jnp.bfloat16)


def local(spectra, send_blocks, tile_slots):
    windows, owners = lax.axis_size("win"), lax.axis_size("pair")
    blocks, _, parts, channels, bins = spectra.shape
    tiles = tile_slots.shape[0]
    groups = channels // GROUP
    exchange = lambda x: lax.all_to_all(x, "pair", split_axis=0, concat_axis=0, tiled=True)
    pieces = (parts, bins // LANES, groups, tiles, GROUP, LANES)

    win = lax.axis_index("win").astype(jnp.int32).reshape(1)
    outgoing = whiten_spread(win, spectra, send_blocks[0].T, tile_slots.T)
    spread = exchange(outgoing.reshape(owners, blocks + 1, GROUP, LANES))
    spread, table = lax.optimization_barrier((spread, lag_rows_table(bins)))
    second, index = pick_second(spread, tiles)
    first = pick_first(index, spread, tiles)
    turn = [
        (w * owners + j, (w + j) % windows * owners + j)
        for w in range(windows)
        for j in range(owners)
    ]
    first = lax.ppermute(first, ("win", "pair"), turn)
    second = exchange(second)
    second, first = lax.optimization_barrier((second, first))
    b = [second] * windows
    ahead = [(w, (w + 1) % windows) for w in range(windows)]
    behind = [(w, (w - 1) % windows) for w in range(windows)]
    for distance in range(1, windows // 2 + 1):
        b[distance] = lax.ppermute(b[distance - 1], "win", ahead)
    for distance in range(windows - 1, windows // 2, -1):
        b[distance] = lax.ppermute(b[(distance + 1) % windows], "win", behind)
    win = settle(win, b[1:2])
    a = exchange(first).reshape(pieces)
    return correlate(win, a, [x.reshape(pieces) for x in b], table)


def solution(mesh):
    in_specs = (P("pair", "win", None, None, None), P("pair", None, None), P("pair", None))
    out_specs = P("win", "pair", None, None)
    return jax.shard_map(local, mesh=mesh, in_specs=in_specs, out_specs=out_specs, check_vma=False)
```

```python
import functools
import math

import jax
import jax.numpy as jnp
from jax import lax
from jax.experimental import pallas as pl
from jax.experimental.pallas import tpu as pltpu
from jax.sharding import PartitionSpec as P

LAGS = 1024
NS = 4096
F0 = 64
BAND = 64
LANES = 128
GROUP = 8
HALF = 64
SETTLE_FLOPS = 8 * 10**9


def whiten_kernel(win_ref, x_ref, out_ref):
    blocks = x_ref.shape[0]
    _, lane_groups, groups = out_ref.shape[:3]
    step = pl.program_id(0)
    row_band = lax.broadcasted_iota(jnp.int32, (LANES, LANES), 0) // BAND
    column_band = lax.broadcasted_iota(jnp.int32, (LANES, LANES), 1) // BAND
    ones = jnp.where(row_band == column_band, 1.0, 0.0).astype(jnp.bfloat16)
    ones = jnp.concatenate([ones, ones, ones], axis=0)
    for lane_group in range(lane_groups):
        lanes = slice(lane_group * LANES, (lane_group + 1) * LANES)
        real = x_ref[:, 0, 0, :, lanes].astype(jnp.float32).reshape(blocks * 16, LANES)
        imag = x_ref[:, 0, 1, :, lanes].astype(jnp.float32).reshape(blocks * 16, LANES)
        rest = real * real + imag * imag
        terms = []
        for _ in range(3):
            terms.append(rest.astype(jnp.bfloat16))
            rest = rest - terms[-1].astype(jnp.float32)
        power = jnp.dot(jnp.concatenate(terms, axis=1), ones, preferred_element_type=jnp.float32)
        scale = lax.rsqrt(power * (1.0 / (2 * BAND)) + 1e-06)
        for part, rows in enumerate((real * scale, imag * scale)):
            rows = rows.reshape(blocks, 2, GROUP, LANES)
            for half in range(2):
                place = lax.rem(2 * step + half + groups - win_ref[0], groups)
                out_ref[part, lane_group, place] = rows[:, half].astype(jnp.bfloat16)


def whiten_spread(win, spectra):
    blocks, _, parts, channels, bins = spectra.shape
    shape = (parts, bins // LANES, channels // GROUP, blocks, GROUP, LANES)
    return pl.pallas_call(
        whiten_kernel,
        grid=(channels // 16,),
        in_specs=[
            pl.BlockSpec(memory_space=pltpu.SMEM),
            pl.BlockSpec((blocks, 1, parts, 16, bins), lambda g: (0, 0, 0, g, 0)),
        ],
        out_specs=pl.BlockSpec(shape, lambda g: (0,) * len(shape)),
        out_shape=jax.ShapeDtypeStruct(shape, jnp.bfloat16),
        compiler_params=pltpu.CompilerParams(vmem_limit_bytes=60 * 2**20),
        name="whiten_spread",
    )(win, spectra)


def copy_pieces(place_ref, x_ref, out_ref, start):
    flat = x_ref.reshape((x_ref.shape[0] * x_ref.shape[1],) + x_ref.shape[2:])

    def one_owner(owner, carry):
        for tile in range(out_ref.shape[1]):
            out_ref[owner, tile] = flat[place_ref[owner, start + tile]]
        return carry

    lax.fori_loop(0, out_ref.shape[0], one_owner, 0, unroll=4)


def places_kernel(tiles, stride, me_ref, near_ref, places_ref, table_ref):
    owners = near_ref.shape[0]
    for owner in range(owners):
        table_ref[4 * owner : 4 * owner + 4, :] = near_ref[me_ref[0] ^ owner]
    sent = [table_ref[pl.ds(k, owners, stride=4), :] for k in range(2)]
    lane = lax.broadcasted_iota(jnp.int32, (owners, LANES), 1)
    by_owner = jnp.concatenate(sent, axis=0).T[:owners].astype(jnp.int32)
    by_owner = by_owner + stride * (lane % HALF)
    places = jnp.zeros((owners, LANES), jnp.int32)
    for part in range(2):
        slots = table_ref[pl.ds(2 + part, owners, stride=4), :].astype(jnp.int32)
        for tile in range(tiles):
            slot = slots[:, tile : tile + 1]
            hit = lane == (slot % 2) * HALF + slot // 2
            place = jnp.sum(jnp.where(hit, by_owner, 0), axis=1, keepdims=True)
            places = jnp.where(lane == part * tiles + tile, place, places)
    places_ref[...] = places


def find_places(near, tiles, stride):
    owners = near.shape[0]
    me = lax.axis_index("pair").astype(jnp.int32).reshape(1)
    return pl.pallas_call(
        functools.partial(places_kernel, tiles, stride),
        in_specs=[
            pl.BlockSpec(memory_space=pltpu.SMEM),
            pl.BlockSpec(memory_space=pltpu.VMEM),
        ],
        out_specs=pl.BlockSpec(memory_space=pltpu.VMEM),
        out_shape=jax.ShapeDtypeStruct((owners, LANES), jnp.int32),
        scratch_shapes=[pltpu.VMEM((owners * 4, LANES), jnp.float32)],
        compiler_params=pltpu.CompilerParams(vmem_limit_bytes=8 * 2**20),
        name="find_places",
    )(me, near)


def pick(index, spread, tiles, start):
    owners = spread.shape[0]
    return pl.pallas_call(
        lambda place_ref, x_ref, out_ref: copy_pieces(place_ref, x_ref, out_ref, start),
        in_specs=[
            pl.BlockSpec(memory_space=pltpu.SMEM),
            pl.BlockSpec(memory_space=pltpu.VMEM),
        ],
        out_specs=pl.BlockSpec(memory_space=pltpu.VMEM),
        out_shape=jax.ShapeDtypeStruct((owners, tiles, GROUP, LANES), jnp.bfloat16),
        compiler_params=pltpu.CompilerParams(vmem_limit_bytes=24 * 2**20),
        name="pick_second" if start else "pick_first",
    )(index, spread)


def share_tables(send_blocks, tile_slots, strides):
    owners = lax.axis_size("pair")
    rows = [send_blocks[0].T, tile_slots.T]
    rows = [jnp.pad(x.astype(jnp.float32), ((0, 0), (0, LANES - x.shape[1]))) for x in rows]
    near = jnp.concatenate(rows, axis=0)[None]
    step = 1
    for size in strides:
        parts = [near]
        for k in range(1, size):
            turn = [(j, j ^ (k * step)) for j in range(owners)]
            parts.append(lax.ppermute(near, "pair", turn))
        near = jnp.concatenate(parts, axis=0)
        step *= size
    return near


def correlate_kernel(scaling, win_ref, a_ref, *refs):
    windows = a_ref.shape[2]
    b_refs, table_hbm = refs[:windows], refs[windows]
    out_ref, stack_ref, table_ref, sem = refs[windows + 1 :]
    step = pl.program_id(0)
    last = pl.num_programs(0) - 1
    _, lane_groups, groups = b_refs[0].shape[:3]
    bins = lane_groups * LANES
    channels = groups * GROUP
    places = [
        [lax.rem(group + distance + groups - win_ref[0], groups) for group in range(groups)]
        for distance in range(windows)
    ]
    table_copy = pltpu.make_async_copy(table_hbm, table_ref, sem)

    def cross(lane_group, slot):
        lanes = lane_group * LANES
        a = [
            [a_ref[part, lane_group, w, step].astype(jnp.float32) for part in range(2)]
            for w in range(windows)
        ]
        for pair in range(groups // 2):
            b = [
                [
                    [
                        b_refs[w][part, lane_group, places[w][pair * 2 + half], step].astype(
                            jnp.float32
                        )
                        for part in range(2)
                    ]
                    for w in range(windows)
                ]
                for half in range(2)
            ]
            for i in range(GROUP):
                rows = [[None, None], [None, None]]
                for w in range(windows):
                    a0 = jnp.broadcast_to(a[w][0][i : i + 1], (GROUP, LANES))
                    a1 = jnp.broadcast_to(a[w][1][i : i + 1], (GROUP, LANES))
                    for half in range(2):
                        b0, b1 = b[half][w]
                        real = a0 * b0 + a1 * b1
                        imag = a1 * b0 - a0 * b1
                        if w:
                            real += rows[half][0]
                            imag += rows[half][1]
                        rows[half] = [real, imag]
                start = i * channels + pair * 2 * GROUP
                for part in range(2):
                    joined = jnp.concatenate([rows[0][part], rows[1][part]], axis=0)
                    stack_ref[
                        slot, start : start + 2 * GROUP, pl.ds(part * bins + lanes, LANES)
                    ] = joined.astype(jnp.bfloat16)

    def lagged(chunk, slot):
        columns = pl.ds(chunk * 2 * LANES, 2 * LANES)
        rows = jnp.dot(stack_ref[slot], table_ref[:, columns], preferred_element_type=jnp.float32)
        rows = (rows * scaling).astype(jnp.bfloat16)
        out_ref[:, 0, :, columns] = rows.reshape(GROUP, channels, 2 * LANES)

    def run(with_cross, with_lagged):
        for chunk in range(lane_groups // 2):
            if with_lagged:
                lagged(chunk, lax.rem(step + 1, 2))
            if with_cross:
                cross(chunk * 2, lax.rem(step, 2))
                cross(chunk * 2 + 1, lax.rem(step, 2))

    @pl.when(step == 0)
    def _():
        table_copy.start()
        run(True, False)
        table_copy.wait()

    @pl.when(jnp.logical_and(step > 0, step < last))
    def _():
        run(True, True)

    @pl.when(step == last)
    def _():
        run(False, True)


def correlate(win, a, b, table):
    _, lane_groups, windows, tiles = a.shape[:4]
    channels = b[0].shape[2] * GROUP
    bins = lane_groups * LANES
    lags = table.shape[1]
    scaling = 1.0 / math.sqrt(windows * bins)
    whole = lambda x: pl.BlockSpec(x.shape, lambda t: (0,) * len(x.shape))
    return pl.pallas_call(
        functools.partial(correlate_kernel, scaling),
        grid=(tiles + 1,),
        in_specs=[pl.BlockSpec(memory_space=pltpu.SMEM)]
        + [whole(x) for x in (a, *b)]
        + [pl.BlockSpec(memory_space=pltpu.HBM)],
        out_specs=pl.BlockSpec(
            (GROUP, 1, channels, lags), lambda t: (0, jnp.maximum(t - 1, 0), 0, 0)
        ),
        out_shape=jax.ShapeDtypeStruct((GROUP, tiles, channels, lags), jnp.bfloat16),
        scratch_shapes=[
            pltpu.VMEM((2, GROUP * channels, 2 * bins), jnp.bfloat16),
            pltpu.VMEM(table.shape, table.dtype),
            pltpu.SemaphoreType.DMA,
        ],
        compiler_params=pltpu.CompilerParams(vmem_limit_bytes=48 * 2**20),
        name="correlate",
    )(win, a, *b, table)


def settle_kernel(win_ref, *refs):
    refs[-1][0] = win_ref[0]


def settle(win, arrays):
    return pl.pallas_call(
        settle_kernel,
        in_specs=[pl.BlockSpec(memory_space=pltpu.SMEM)]
        + [pl.BlockSpec(memory_space=pl.ANY)] * len(arrays),
        out_specs=pl.BlockSpec(memory_space=pltpu.SMEM),
        out_shape=jax.ShapeDtypeStruct(win.shape, win.dtype),
        compiler_params=pltpu.CompilerParams(vmem_limit_bytes=2**20),
        cost_estimate=pl.CostEstimate(flops=SETTLE_FLOPS, bytes_accessed=0, transcendentals=0),
        name="settle",
    )(win, *arrays)


def lag_rows_table(bin_total):
    fine = 16
    lag_index = jnp.arange(LAGS, dtype=jnp.int32) - LAGS // 2

    def turns(bins):
        wrapped = bins[:, None] * lag_index[None, :] % NS
        phases = wrapped.astype(jnp.float32) * (2.0 * math.pi / NS)
        return jnp.cos(phases), jnp.sin(phases)

    coarse_bins = jnp.arange(bin_total // fine, dtype=jnp.int32) * fine + F0
    pairs = turns(jnp.concatenate([coarse_bins, jnp.arange(fine, dtype=jnp.int32)]))
    cosine, sine = lax.optimization_barrier(pairs)
    coarse = [x[:-fine, None, :] for x in (cosine, sine)]
    small = [x[None, -fine:, :] for x in (cosine, sine)]
    real = coarse[0] * small[0] - coarse[1] * small[1]
    imag = coarse[1] * small[0] + coarse[0] * small[1]
    table = jnp.stack([real, -imag]).astype(jnp.bfloat16)
    return table.reshape(2 * bin_total, LAGS)


def local(spectra, send_blocks, tile_slots):
    windows, owners = lax.axis_size("win"), lax.axis_size("pair")
    blocks, _, parts, channels, bins = spectra.shape
    tiles = tile_slots.shape[0]
    groups = channels // GROUP
    exchange = lambda x: lax.all_to_all(x, "pair", split_axis=0, concat_axis=0, tiled=True)
    pieces = (parts, bins // LANES, groups, tiles, GROUP, LANES)

    win = lax.axis_index("win").astype(jnp.int32).reshape(1)
    outgoing = whiten_spread(win, spectra)
    outgoing, *tables = lax.optimization_barrier((outgoing, send_blocks, tile_slots))
    spread = exchange(outgoing.reshape(owners, blocks, GROUP, LANES))
    near = share_tables(*tables, (2, 8, owners // 16))
    index = find_places(near, tiles, blocks)
    spread, index, table = lax.optimization_barrier((spread, index, lag_rows_table(bins)))
    second = pick(index, spread, tiles, tiles)
    first = pick(index, spread, tiles, 0)
    turn = [
        (w * owners + j, (w + j) % windows * owners + j)
        for w in range(windows)
        for j in range(owners)
    ]
    first = lax.ppermute(first, ("win", "pair"), turn)
    second = exchange(second)
    second, first = lax.optimization_barrier((second, first))
    b = [second]
    for distance in range(1, windows):
        step = [(w, (w + distance) % windows) for w in range(windows)]
        b.append(lax.ppermute(second, "win", step))
    win = settle(win, b[windows // 2 : windows // 2 + 1])
    a = exchange(first).reshape(pieces)
    return correlate(win, a, [x.reshape(pieces) for x in b], table)


def solution(mesh):
    in_specs = (P("pair", "win", None, None, None), P("pair", None, None), P("pair", None))
    out_specs = P("win", "pair", None, None)
    return jax.shard_map(local, mesh=mesh, in_specs=in_specs, out_specs=out_specs, check_vma=False)
```

```python
import functools
import math

import jax
import jax.numpy as jnp
from jax import lax
from jax.experimental import pallas as pl
from jax.experimental.pallas import tpu as pltpu
from jax.sharding import PartitionSpec as P

LAGS = 1024
NS = 4096
F0 = 64
BAND = 64
LANES = 128
GROUP = 8
HALF = 64
SETTLE_FLOPS = 8 * 10**9


def whiten_kernel(win_ref, x_ref, sent_ref, slots_ref, out_ref, table_ref):
    blocks, _, _, channels, _ = x_ref.shape
    _, lane_groups, groups = out_ref.shape[:3]
    row_band = lax.broadcasted_iota(jnp.int32, (LANES, LANES), 0) // BAND
    column_band = lax.broadcasted_iota(jnp.int32, (LANES, LANES), 1) // BAND
    ones = jnp.where(row_band == column_band, 1.0, 0.0).astype(jnp.bfloat16)
    ones = jnp.concatenate([ones, ones, ones], axis=0)
    places = [lax.rem(group + groups - win_ref[0], groups) for group in range(groups)]
    for lane_group in range(lane_groups):
        lanes = slice(lane_group * LANES, (lane_group + 1) * LANES)
        real, imag = [
            x_ref[:, 0, part, :, lanes].astype(jnp.float32).reshape(blocks * channels, LANES)
            for part in range(2)
        ]
        rest = real * real + imag * imag
        terms = []
        for _ in range(3):
            terms.append(rest.astype(jnp.bfloat16))
            rest = rest - terms[-1].astype(jnp.float32)
        power = jnp.dot(jnp.concatenate(terms, axis=1), ones, preferred_element_type=jnp.float32)
        scale = lax.rsqrt(power * (1.0 / (2 * BAND)) + 1e-06)
        for part, rows in enumerate((real * scale, imag * scale)):
            rows = rows.reshape(blocks, groups, GROUP, LANES)
            for group in range(groups):
                out_ref[part, lane_group, places[group], :blocks] = rows[:, group].astype(
                    jnp.bfloat16
                )

    @pl.when(pl.program_id(0) == 0)
    def _():
        table_ref[...] = jnp.zeros_like(table_ref)
        table_ref[0:2, : sent_ref.shape[1]] = sent_ref[...].astype(jnp.float32)
        table_ref[2:4, : slots_ref.shape[1]] = slots_ref[...].astype(jnp.float32)

    piece = table_ref[...].astype(jnp.bfloat16)
    shape = out_ref.shape
    out_ref[:, :, :, blocks] = jnp.broadcast_to(piece, shape[:3] + shape[4:])


def whiten_spread(win, spectra, sent, slots):
    blocks, _, parts, channels, bins = spectra.shape
    shape = (parts, bins // LANES, channels // GROUP, blocks + 1, GROUP, LANES)
    steps = 2
    width = bins // steps
    return pl.pallas_call(
        whiten_kernel,
        grid=(steps,),
        in_specs=[
            pl.BlockSpec(memory_space=pltpu.SMEM),
            pl.BlockSpec((blocks, 1, parts, channels, width), lambda g: (0, 0, 0, 0, g)),
            pl.BlockSpec(sent.shape, lambda g: (0, 0)),
            pl.BlockSpec(slots.shape, lambda g: (0, 0)),
        ],
        out_specs=pl.BlockSpec(
            (parts, width // LANES) + shape[2:], lambda g: (0, g, 0, 0, 0, 0)
        ),
        out_shape=jax.ShapeDtypeStruct(shape, jnp.bfloat16),
        scratch_shapes=[pltpu.VMEM((GROUP, LANES), jnp.float32)],
        compiler_params=pltpu.CompilerParams(vmem_limit_bytes=60 * 2**20),
        name="whiten_spread",
    )(win, spectra, sent, slots)


def copy_pieces(place_ref, x_ref, out_ref, start):
    flat = x_ref.reshape((x_ref.shape[0] * x_ref.shape[1],) + x_ref.shape[2:])

    def one_owner(owner, carry):
        for tile in range(out_ref.shape[1]):
            out_ref[owner, tile] = flat[place_ref[start + tile, owner]]
        return carry

    lax.fori_loop(0, out_ref.shape[0], one_owner, 0, unroll=4)


def pick_second_kernel(x_ref, out_ref, index_ref, table_ref, place_ref, sem):
    owners, stride = x_ref.shape[:2]
    tiles = out_ref.shape[1]
    table_ref[...] = x_ref[:, stride - 1].astype(jnp.float32).reshape(table_ref.shape)
    sent = [table_ref[pl.ds(k, owners, stride=GROUP), :] for k in range(2)]
    lane = lax.broadcasted_iota(jnp.int32, (owners, LANES), 1)
    by_owner = jnp.concatenate(sent, axis=0).T[:owners].astype(jnp.int32)
    by_owner = by_owner + stride * (lane % HALF)
    places = jnp.zeros((owners, LANES), jnp.int32)
    for part in range(2):
        slots = table_ref[pl.ds(2 + part, owners, stride=GROUP), :].astype(jnp.int32)
        for tile in range(tiles):
            slot = slots[:, tile : tile + 1]
            hit = lane == (slot % 2) * HALF + slot // 2
            place = jnp.sum(jnp.where(hit, by_owner, 0), axis=1, keepdims=True)
            places = jnp.where(lane == part * tiles + tile, place, places)
    wide = jnp.concatenate([places, places], axis=0).astype(jnp.float32).T
    index_ref[...] = wide[: 2 * tiles].astype(jnp.int32)
    copy = pltpu.make_async_copy(index_ref, place_ref, sem)
    copy.start()
    copy.wait()
    copy_pieces(place_ref, x_ref, out_ref, tiles)


def pick_second(spread, tiles):
    owners = spread.shape[0]
    return pl.pallas_call(
        pick_second_kernel,
        in_specs=[pl.BlockSpec(memory_space=pltpu.VMEM)],
        out_specs=[pl.BlockSpec(memory_space=pltpu.VMEM)] * 2,
        out_shape=[
            jax.ShapeDtypeStruct((owners, tiles, GROUP, LANES), jnp.bfloat16),
            jax.ShapeDtypeStruct((2 * tiles, LANES), jnp.int32),
        ],
        scratch_shapes=[
            pltpu.VMEM((owners * GROUP, LANES), jnp.float32),
            pltpu.SMEM((2 * tiles, LANES), jnp.int32),
            pltpu.SemaphoreType.DMA,
        ],
        compiler_params=pltpu.CompilerParams(vmem_limit_bytes=24 * 2**20),
        name="pick_second",
    )(spread)


def pick_first(index, spread, tiles):
    owners = spread.shape[0]
    return pl.pallas_call(
        lambda place_ref, x_ref, out_ref: copy_pieces(place_ref, x_ref, out_ref, 0),
        in_specs=[
            pl.BlockSpec(memory_space=pltpu.SMEM),
            pl.BlockSpec(memory_space=pltpu.VMEM),
        ],
        out_specs=pl.BlockSpec(memory_space=pltpu.VMEM),
        out_shape=jax.ShapeDtypeStruct((owners, tiles, GROUP, LANES), jnp.bfloat16),
        compiler_params=pltpu.CompilerParams(vmem_limit_bytes=24 * 2**20),
        name="pick_first",
    )(index, spread)


def correlate_kernel(scaling, win_ref, a_ref, *refs):
    windows = a_ref.shape[2]
    b_refs, table_hbm = refs[:windows], refs[windows]
    out_ref, stack_ref, table_ref, sem = refs[windows + 1 :]
    step = pl.program_id(0)
    last = pl.num_programs(0) - 1
    _, lane_groups, groups = b_refs[0].shape[:3]
    bins = lane_groups * LANES
    channels = groups * GROUP
    places = [
        [lax.rem(group + distance + groups - win_ref[0], groups) for group in range(groups)]
        for distance in range(windows)
    ]
    table_copy = pltpu.make_async_copy(table_hbm, table_ref, sem)

    def cross(lane_group, slot):
        lanes = lane_group * LANES
        a = [
            [a_ref[part, lane_group, w, step].astype(jnp.float32) for part in range(2)]
            for w in range(windows)
        ]
        for pair in range(groups // 2):
            b = [
                [
                    [
                        b_refs[w][part, lane_group, places[w][pair * 2 + half], step].astype(
                            jnp.float32
                        )
                        for part in range(2)
                    ]
                    for w in range(windows)
                ]
                for half in range(2)
            ]
            for i in range(GROUP):
                rows = [[None, None], [None, None]]
                for w in range(windows):
                    a0 = jnp.broadcast_to(a[w][0][i : i + 1], (GROUP, LANES))
                    a1 = jnp.broadcast_to(a[w][1][i : i + 1], (GROUP, LANES))
                    for half in range(2):
                        b0, b1 = b[half][w]
                        real = a0 * b0 + a1 * b1
                        imag = a1 * b0 - a0 * b1
                        if w:
                            real += rows[half][0]
                            imag += rows[half][1]
                        rows[half] = [real, imag]
                start = i * channels + pair * 2 * GROUP
                for part in range(2):
                    joined = jnp.concatenate([rows[0][part], rows[1][part]], axis=0)
                    stack_ref[
                        slot, start : start + 2 * GROUP, pl.ds(part * bins + lanes, LANES)
                    ] = joined.astype(jnp.bfloat16)

    def lagged(chunk, slot):
        columns = pl.ds(chunk * 2 * LANES, 2 * LANES)
        rows = jnp.dot(stack_ref[slot], table_ref[:, columns], preferred_element_type=jnp.float32)
        rows = (rows * scaling).astype(jnp.bfloat16)
        out_ref[:, 0, :, columns] = rows.reshape(GROUP, channels, 2 * LANES)

    def run(with_cross, with_lagged):
        for chunk in range(lane_groups // 2):
            if with_lagged:
                lagged(chunk, lax.rem(step + 1, 2))
            if with_cross:
                cross(chunk * 2, lax.rem(step, 2))
                cross(chunk * 2 + 1, lax.rem(step, 2))

    @pl.when(step == 0)
    def _():
        table_copy.start()
        run(True, False)
        table_copy.wait()

    @pl.when(jnp.logical_and(step > 0, step < last))
    def _():
        run(True, True)

    @pl.when(step == last)
    def _():
        run(False, True)


def correlate(win, a, b, table):
    _, lane_groups, windows, tiles = a.shape[:4]
    channels = b[0].shape[2] * GROUP
    bins = lane_groups * LANES
    lags = table.shape[1]
    scaling = 1.0 / math.sqrt(windows * bins)
    whole = lambda x: pl.BlockSpec(x.shape, lambda t: (0,) * len(x.shape))
    return pl.pallas_call(
        functools.partial(correlate_kernel, scaling),
        grid=(tiles + 1,),
        in_specs=[pl.BlockSpec(memory_space=pltpu.SMEM)]
        + [whole(x) for x in (a, *b)]
        + [pl.BlockSpec(memory_space=pltpu.HBM)],
        out_specs=pl.BlockSpec(
            (GROUP, 1, channels, lags), lambda t: (0, jnp.maximum(t - 1, 0), 0, 0)
        ),
        out_shape=jax.ShapeDtypeStruct((GROUP, tiles, channels, lags), jnp.bfloat16),
        scratch_shapes=[
            pltpu.VMEM((2, GROUP * channels, 2 * bins), jnp.bfloat16),
            pltpu.VMEM(table.shape, table.dtype),
            pltpu.SemaphoreType.DMA,
        ],
        compiler_params=pltpu.CompilerParams(vmem_limit_bytes=48 * 2**20),
        name="correlate",
    )(win, a, *b, table)


def settle_kernel(win_ref, *refs):
    refs[-1][0] = win_ref[0]


def settle(win, arrays):
    return pl.pallas_call(
        settle_kernel,
        in_specs=[pl.BlockSpec(memory_space=pltpu.SMEM)]
        + [pl.BlockSpec(memory_space=pl.ANY)] * len(arrays),
        out_specs=pl.BlockSpec(memory_space=pltpu.SMEM),
        out_shape=jax.ShapeDtypeStruct(win.shape, win.dtype),
        compiler_params=pltpu.CompilerParams(vmem_limit_bytes=2**20),
        cost_estimate=pl.CostEstimate(flops=SETTLE_FLOPS, bytes_accessed=0, transcendentals=0),
        name="settle",
    )(win, *arrays)


def lag_rows_table(bin_total):
    bin_index = jnp.arange(bin_total, dtype=jnp.int32) + F0
    lag_index = jnp.arange(LAGS, dtype=jnp.int32) - LAGS // 2
    wrapped = bin_index[:, None] * lag_index[None, :] % NS
    phases = wrapped.astype(jnp.float32) * (2.0 * math.pi / NS)
    return jnp.concatenate([jnp.cos(phases), -jnp.sin(phases)], axis=0).astype(jnp.bfloat16)


def local(spectra, send_blocks, tile_slots):
    windows, owners = lax.axis_size("win"), lax.axis_size("pair")
    blocks, _, parts, channels, bins = spectra.shape
    tiles = tile_slots.shape[0]
    groups = channels // GROUP
    exchange = lambda x: lax.all_to_all(x, "pair", split_axis=0, concat_axis=0, tiled=True)
    pieces = (parts, bins // LANES, groups, tiles, GROUP, LANES)

    win = lax.axis_index("win").astype(jnp.int32).reshape(1)
    outgoing = whiten_spread(win, spectra, send_blocks[0].T, tile_slots.T)
    spread = exchange(outgoing.reshape(owners, blocks + 1, GROUP, LANES))
    spread, table = lax.optimization_barrier((spread, lag_rows_table(bins)))
    second, index = pick_second(spread, tiles)
    first = pick_first(index, spread, tiles)
    turn = [
        (w * owners + j, (w + j) % windows * owners + j)
        for w in range(windows)
        for j in range(owners)
    ]
    first = lax.ppermute(first, ("win", "pair"), turn)
    second = exchange(second)
    second, first = lax.optimization_barrier((second, first))
    b = [second]
    for distance in range(1, windows):
        step = [(w, (w + distance) % windows) for w in range(windows)]
        b.append(lax.ppermute(second, "win", step))
    win = settle(win, b[windows // 2 : windows // 2 + 1])
    a = exchange(first).reshape(pieces)
    return correlate(win, a, [x.reshape(pieces) for x in b], table)


def solution(mesh):
    in_specs = (P("pair", "win", None, None, None), P("pair", None, None), P("pair", None))
    out_specs = P("win", "pair", None, None)
    return jax.shard_map(local, mesh=mesh, in_specs=in_specs, out_specs=out_specs, check_vma=False)
```

```python
import functools
import math

import jax
import jax.numpy as jnp
from jax import lax
from jax.experimental import pallas as pl
from jax.experimental.pallas import tpu as pltpu
from jax.sharding import PartitionSpec as P

LAGS = 1024
NS = 4096
F0 = 64
BAND = 64
LANES = 128
GROUP = 8
HALF = 64
SETTLE_FLOPS = 8 * 10**9


def whiten_kernel(win_ref, x_ref, sent_ref, slots_ref, out_ref, table_ref):
    blocks, _, _, channels, _ = x_ref.shape
    _, lane_groups, groups = out_ref.shape[:3]
    row_band = lax.broadcasted_iota(jnp.int32, (LANES, LANES), 0) // BAND
    column_band = lax.broadcasted_iota(jnp.int32, (LANES, LANES), 1) // BAND
    ones = jnp.where(row_band == column_band, 1.0, 0.0).astype(jnp.bfloat16)
    ones = jnp.concatenate([ones, ones, ones], axis=0)
    places = [lax.rem(group + groups - win_ref[0], groups) for group in range(groups)]
    for lane_group in range(lane_groups):
        lanes = slice(lane_group * LANES, (lane_group + 1) * LANES)
        real, imag = [
            x_ref[:, 0, part, :, lanes].astype(jnp.float32).reshape(blocks * channels, LANES)
            for part in range(2)
        ]
        rest = real * real + imag * imag
        terms = []
        for _ in range(3):
            terms.append(rest.astype(jnp.bfloat16))
            rest = rest - terms[-1].astype(jnp.float32)
        power = jnp.dot(jnp.concatenate(terms, axis=1), ones, preferred_element_type=jnp.float32)
        scale = lax.rsqrt(power * (1.0 / (2 * BAND)) + 1e-06)
        for part, rows in enumerate((real * scale, imag * scale)):
            rows = rows.reshape(blocks, groups, GROUP, LANES)
            for group in range(groups):
                out_ref[part, lane_group, places[group], :blocks] = rows[:, group].astype(
                    jnp.bfloat16
                )

    @pl.when(pl.program_id(0) == 0)
    def _():
        table_ref[...] = jnp.zeros_like(table_ref)
        table_ref[0:2, : sent_ref.shape[1]] = sent_ref[...].astype(jnp.float32)
        table_ref[2:4, : slots_ref.shape[1]] = slots_ref[...].astype(jnp.float32)

    piece = table_ref[...].astype(jnp.bfloat16)
    shape = out_ref.shape
    out_ref[:, :, :, blocks] = jnp.broadcast_to(piece, shape[:3] + shape[4:])


def whiten_spread(win, spectra, sent, slots):
    blocks, _, parts, channels, bins = spectra.shape
    shape = (parts, bins // LANES, channels // GROUP, blocks + 1, GROUP, LANES)
    steps = 2
    width = bins // steps
    return pl.pallas_call(
        whiten_kernel,
        grid=(steps,),
        in_specs=[
            pl.BlockSpec(memory_space=pltpu.SMEM),
            pl.BlockSpec((blocks, 1, parts, channels, width), lambda g: (0, 0, 0, 0, g)),
            pl.BlockSpec(sent.shape, lambda g: (0, 0)),
            pl.BlockSpec(slots.shape, lambda g: (0, 0)),
        ],
        out_specs=pl.BlockSpec(
            (parts, width // LANES) + shape[2:], lambda g: (0, g, 0, 0, 0, 0)
        ),
        out_shape=jax.ShapeDtypeStruct(shape, jnp.bfloat16),
        scratch_shapes=[pltpu.VMEM((GROUP, LANES), jnp.float32)],
        compiler_params=pltpu.CompilerParams(vmem_limit_bytes=60 * 2**20),
        name="whiten_spread",
    )(win, spectra, sent, slots)


def copy_pieces(place_ref, x_ref, out_ref, start):
    flat = x_ref.reshape((x_ref.shape[0] * x_ref.shape[1],) + x_ref.shape[2:])

    def one_owner(owner, carry):
        for tile in range(out_ref.shape[1]):
            out_ref[owner, tile] = flat[place_ref[start + tile, owner]]
        return carry

    lax.fori_loop(0, out_ref.shape[0], one_owner, 0, unroll=4)


def pick_second_kernel(x_ref, out_ref, index_ref, table_ref, place_ref, sem):
    owners, stride = x_ref.shape[:2]
    tiles = out_ref.shape[1]
    table_ref[...] = x_ref[:, stride - 1].astype(jnp.float32).reshape(table_ref.shape)
    sent = [table_ref[pl.ds(k, owners, stride=GROUP), :] for k in range(2)]
    lane = lax.broadcasted_iota(jnp.int32, (owners, LANES), 1)
    by_owner = jnp.concatenate(sent, axis=0).T[:owners].astype(jnp.int32)
    by_owner = by_owner + stride * (lane % HALF)
    places = jnp.zeros((owners, LANES), jnp.int32)
    for part in range(2):
        slots = table_ref[pl.ds(2 + part, owners, stride=GROUP), :].astype(jnp.int32)
        for tile in range(tiles):
            slot = slots[:, tile : tile + 1]
            hit = lane == (slot % 2) * HALF + slot // 2
            place = jnp.sum(jnp.where(hit, by_owner, 0), axis=1, keepdims=True)
            places = jnp.where(lane == part * tiles + tile, place, places)
    wide = jnp.concatenate([places, places], axis=0).astype(jnp.float32).T
    index_ref[...] = wide[: 2 * tiles].astype(jnp.int32)
    copy = pltpu.make_async_copy(index_ref, place_ref, sem)
    copy.start()
    copy.wait()
    copy_pieces(place_ref, x_ref, out_ref, tiles)


def pick_second(spread, tiles):
    owners = spread.shape[0]
    return pl.pallas_call(
        pick_second_kernel,
        in_specs=[pl.BlockSpec(memory_space=pltpu.VMEM)],
        out_specs=[pl.BlockSpec(memory_space=pltpu.VMEM)] * 2,
        out_shape=[
            jax.ShapeDtypeStruct((owners, tiles, GROUP, LANES), jnp.bfloat16),
            jax.ShapeDtypeStruct((2 * tiles, LANES), jnp.int32),
        ],
        scratch_shapes=[
            pltpu.VMEM((owners * GROUP, LANES), jnp.float32),
            pltpu.SMEM((2 * tiles, LANES), jnp.int32),
            pltpu.SemaphoreType.DMA,
        ],
        compiler_params=pltpu.CompilerParams(vmem_limit_bytes=24 * 2**20),
        name="pick_second",
    )(spread)


def pick_first(index, spread, tiles):
    owners = spread.shape[0]
    return pl.pallas_call(
        lambda place_ref, x_ref, out_ref: copy_pieces(place_ref, x_ref, out_ref, 0),
        in_specs=[
            pl.BlockSpec(memory_space=pltpu.SMEM),
            pl.BlockSpec(memory_space=pltpu.VMEM),
        ],
        out_specs=pl.BlockSpec(memory_space=pltpu.VMEM),
        out_shape=jax.ShapeDtypeStruct((owners, tiles, GROUP, LANES), jnp.bfloat16),
        compiler_params=pltpu.CompilerParams(vmem_limit_bytes=24 * 2**20),
        name="pick_first",
    )(index, spread)


def correlate_kernel(scaling, win_ref, a_ref, *refs):
    windows = a_ref.shape[2]
    b_refs, table_hbm = refs[:windows], refs[windows]
    out_ref, stack_ref, table_ref, sem = refs[windows + 1 :]
    step = pl.program_id(0)
    last = pl.num_programs(0) - 1
    _, lane_groups, groups = b_refs[0].shape[:3]
    bins = lane_groups * LANES
    channels = groups * GROUP
    places = [
        [lax.rem(group + distance + groups - win_ref[0], groups) for group in range(groups)]
        for distance in range(windows)
    ]
    table_copy = pltpu.make_async_copy(table_hbm, table_ref, sem)

    def cross(lane_group, slot):
        lanes = lane_group * LANES
        a = [
            [a_ref[part, lane_group, w, step].astype(jnp.float32) for part in range(2)]
            for w in range(windows)
        ]
        for pair in range(groups // 2):
            b = [
                [
                    [
                        b_refs[w][part, lane_group, places[w][pair * 2 + half], step].astype(
                            jnp.float32
                        )
                        for part in range(2)
                    ]
                    for w in range(windows)
                ]
                for half in range(2)
            ]
            for i in range(GROUP):
                rows = [[None, None], [None, None]]
                for w in range(windows):
                    a0 = jnp.broadcast_to(a[w][0][i : i + 1], (GROUP, LANES))
                    a1 = jnp.broadcast_to(a[w][1][i : i + 1], (GROUP, LANES))
                    for half in range(2):
                        b0, b1 = b[half][w]
                        real = a0 * b0 + a1 * b1
                        imag = a1 * b0 - a0 * b1
                        if w:
                            real += rows[half][0]
                            imag += rows[half][1]
                        rows[half] = [real, imag]
                start = i * channels + pair * 2 * GROUP
                for part in range(2):
                    joined = jnp.concatenate([rows[0][part], rows[1][part]], axis=0)
                    stack_ref[
                        slot, start : start + 2 * GROUP, pl.ds(part * bins + lanes, LANES)
                    ] = joined.astype(jnp.bfloat16)

    def lagged(chunk, slot):
        columns = pl.ds(chunk * 2 * LANES, 2 * LANES)
        rows = jnp.dot(stack_ref[slot], table_ref[:, columns], preferred_element_type=jnp.float32)
        rows = (rows * scaling).astype(jnp.bfloat16)
        out_ref[:, 0, :, columns] = rows.reshape(GROUP, channels, 2 * LANES)

    def run(with_cross, with_lagged):
        for chunk in range(lane_groups // 2):
            if with_lagged:
                lagged(chunk, lax.rem(step + 1, 2))
            if with_cross:
                cross(chunk * 2, lax.rem(step, 2))
                cross(chunk * 2 + 1, lax.rem(step, 2))

    @pl.when(step == 0)
    def _():
        table_copy.start()
        run(True, False)
        table_copy.wait()

    @pl.when(jnp.logical_and(step > 0, step < last))
    def _():
        run(True, True)

    @pl.when(step == last)
    def _():
        run(False, True)


def correlate(win, a, b, table):
    _, lane_groups, windows, tiles = a.shape[:4]
    channels = b[0].shape[2] * GROUP
    bins = lane_groups * LANES
    lags = table.shape[1]
    scaling = 1.0 / math.sqrt(windows * bins)
    whole = lambda x: pl.BlockSpec(x.shape, lambda t: (0,) * len(x.shape))
    return pl.pallas_call(
        functools.partial(correlate_kernel, scaling),
        grid=(tiles + 1,),
        in_specs=[pl.BlockSpec(memory_space=pltpu.SMEM)]
        + [whole(x) for x in (a, *b)]
        + [pl.BlockSpec(memory_space=pltpu.HBM)],
        out_specs=pl.BlockSpec(
            (GROUP, 1, channels, lags), lambda t: (0, jnp.maximum(t - 1, 0), 0, 0)
        ),
        out_shape=jax.ShapeDtypeStruct((GROUP, tiles, channels, lags), jnp.bfloat16),
        scratch_shapes=[
            pltpu.VMEM((2, GROUP * channels, 2 * bins), jnp.bfloat16),
            pltpu.VMEM(table.shape, table.dtype),
            pltpu.SemaphoreType.DMA,
        ],
        compiler_params=pltpu.CompilerParams(vmem_limit_bytes=48 * 2**20),
        name="correlate",
    )(win, a, *b, table)


def settle_kernel(win_ref, *refs):
    refs[-1][0] = win_ref[0]


def settle(win, arrays):
    return pl.pallas_call(
        settle_kernel,
        in_specs=[pl.BlockSpec(memory_space=pltpu.SMEM)]
        + [pl.BlockSpec(memory_space=pl.ANY)] * len(arrays),
        out_specs=pl.BlockSpec(memory_space=pltpu.SMEM),
        out_shape=jax.ShapeDtypeStruct(win.shape, win.dtype),
        compiler_params=pltpu.CompilerParams(vmem_limit_bytes=2**20),
        cost_estimate=pl.CostEstimate(flops=SETTLE_FLOPS, bytes_accessed=0, transcendentals=0),
        name="settle",
    )(win, *arrays)


def lag_rows_table(bin_total):
    bin_index = jnp.arange(bin_total, dtype=jnp.int32) + F0
    lag_index = jnp.arange(LAGS, dtype=jnp.int32) - LAGS // 2
    wrapped = bin_index[:, None] * lag_index[None, :] % NS
    phases = wrapped.astype(jnp.float32) * (2.0 * math.pi / NS)
    return jnp.concatenate([jnp.cos(phases), -jnp.sin(phases)], axis=0).astype(jnp.bfloat16)


def local(spectra, send_blocks, tile_slots):
    windows, owners = lax.axis_size("win"), lax.axis_size("pair")
    blocks, _, parts, channels, bins = spectra.shape
    tiles = tile_slots.shape[0]
    groups = channels // GROUP
    exchange = lambda x: lax.all_to_all(x, "pair", split_axis=0, concat_axis=0, tiled=True)
    pieces = (parts, bins // LANES, groups, tiles, GROUP, LANES)

    win = lax.axis_index("win").astype(jnp.int32).reshape(1)
    outgoing = whiten_spread(win, spectra, send_blocks[0].T, tile_slots.T)
    spread = exchange(outgoing.reshape(owners, blocks + 1, GROUP, LANES))
    spread, table = lax.optimization_barrier((spread, lag_rows_table(bins)))
    second, index = pick_second(spread, tiles)
    first = pick_first(index, spread, tiles)
    turn = [
        (w * owners + j, (w + j) % windows * owners + j)
        for w in range(windows)
        for j in range(owners)
    ]
    first = lax.ppermute(first, ("win", "pair"), turn)
    second = exchange(second)
    second, first = lax.optimization_barrier((second, first))
    b = [second]
    for distance in range(1, windows):
        step = [(w, (w + distance) % windows) for w in range(windows)]
        b.append(lax.ppermute(second, "win", step))
    win = settle(win, b[1:2] + b[-1:])
    a = exchange(first).reshape(pieces)
    return correlate(win, a, [x.reshape(pieces) for x in b], table)


def solution(mesh):
    in_specs = (P("pair", "win", None, None, None), P("pair", None, None), P("pair", None))
    out_specs = P("win", "pair", None, None)
    return jax.shard_map(local, mesh=mesh, in_specs=in_specs, out_specs=out_specs, check_vma=False)
```

```python
import functools
import math

import jax
import jax.numpy as jnp
from jax import lax
from jax.experimental import pallas as pl
from jax.experimental.pallas import tpu as pltpu
from jax.sharding import PartitionSpec as P

LAGS = 1024
NS = 4096
F0 = 64
BAND = 64
LANES = 128
GROUP = 8
HALF = 64
SETTLE_FLOPS = 8 * 10**9


def whiten_kernel(win_ref, x_ref, sent_ref, slots_ref, out_ref, table_ref):
    blocks, _, _, channels, _ = x_ref.shape
    _, lane_groups, groups = out_ref.shape[:3]
    row_band = lax.broadcasted_iota(jnp.int32, (LANES, LANES), 0) // BAND
    column_band = lax.broadcasted_iota(jnp.int32, (LANES, LANES), 1) // BAND
    ones = jnp.where(row_band == column_band, 1.0, 0.0).astype(jnp.bfloat16)
    ones = jnp.concatenate([ones, ones, ones], axis=0)
    places = [lax.rem(group + groups - win_ref[0], groups) for group in range(groups)]
    for lane_group in range(lane_groups):
        lanes = slice(lane_group * LANES, (lane_group + 1) * LANES)
        real, imag = [
            x_ref[:, 0, part, :, lanes].astype(jnp.float32).reshape(blocks * channels, LANES)
            for part in range(2)
        ]
        rest = real * real + imag * imag
        terms = []
        for _ in range(3):
            terms.append(rest.astype(jnp.bfloat16))
            rest = rest - terms[-1].astype(jnp.float32)
        power = jnp.dot(jnp.concatenate(terms, axis=1), ones, preferred_element_type=jnp.float32)
        scale = lax.rsqrt(power * (1.0 / (2 * BAND)) + 1e-06)
        for part, rows in enumerate((real * scale, imag * scale)):
            rows = rows.reshape(blocks, groups, GROUP, LANES)
            for group in range(groups):
                out_ref[part, lane_group, places[group], :blocks] = rows[:, group].astype(
                    jnp.bfloat16
                )

    @pl.when(pl.program_id(0) == 0)
    def _():
        table_ref[...] = jnp.zeros_like(table_ref)
        table_ref[0:2, : sent_ref.shape[1]] = sent_ref[...].astype(jnp.float32)
        table_ref[2:4, : slots_ref.shape[1]] = slots_ref[...].astype(jnp.float32)

    piece = table_ref[...].astype(jnp.bfloat16)
    shape = out_ref.shape
    out_ref[:, :, :, blocks] = jnp.broadcast_to(piece, shape[:3] + shape[4:])


def whiten_spread(win, spectra, sent, slots):
    blocks, _, parts, channels, bins = spectra.shape
    shape = (parts, bins // LANES, channels // GROUP, blocks + 1, GROUP, LANES)
    steps = 2
    width = bins // steps
    return pl.pallas_call(
        whiten_kernel,
        grid=(steps,),
        in_specs=[
            pl.BlockSpec(memory_space=pltpu.SMEM),
            pl.BlockSpec((blocks, 1, parts, channels, width), lambda g: (0, 0, 0, 0, g)),
            pl.BlockSpec(sent.shape, lambda g: (0, 0)),
            pl.BlockSpec(slots.shape, lambda g: (0, 0)),
        ],
        out_specs=pl.BlockSpec(
            (parts, width // LANES) + shape[2:], lambda g: (0, g, 0, 0, 0, 0)
        ),
        out_shape=jax.ShapeDtypeStruct(shape, jnp.bfloat16),
        scratch_shapes=[pltpu.VMEM((GROUP, LANES), jnp.float32)],
        compiler_params=pltpu.CompilerParams(vmem_limit_bytes=60 * 2**20),
        name="whiten_spread",
    )(win, spectra, sent, slots)


def copy_pieces(place_ref, x_ref, out_ref, start):
    flat = x_ref.reshape((x_ref.shape[0] * x_ref.shape[1],) + x_ref.shape[2:])

    def one_owner(owner, carry):
        for tile in range(out_ref.shape[1]):
            out_ref[owner, tile] = flat[place_ref[start + tile, owner]]
        return carry

    lax.fori_loop(0, out_ref.shape[0], one_owner, 0, unroll=4)


def pick_second_kernel(x_ref, out_ref, index_ref, table_ref, place_ref, sem):
    owners, stride = x_ref.shape[:2]
    tiles = out_ref.shape[1]
    table_ref[...] = x_ref[:, stride - 1].astype(jnp.float32).reshape(table_ref.shape)
    sent = [table_ref[pl.ds(k, owners, stride=GROUP), :] for k in range(2)]
    lane = lax.broadcasted_iota(jnp.int32, (owners, LANES), 1)
    by_owner = jnp.concatenate(sent, axis=0).T[:owners].astype(jnp.int32)
    by_owner = by_owner + stride * (lane % HALF)
    places = jnp.zeros((owners, LANES), jnp.int32)
    for part in range(2):
        slots = table_ref[pl.ds(2 + part, owners, stride=GROUP), :].astype(jnp.int32)
        for tile in range(tiles):
            slot = slots[:, tile : tile + 1]
            hit = lane == (slot % 2) * HALF + slot // 2
            place = jnp.sum(jnp.where(hit, by_owner, 0), axis=1, keepdims=True)
            places = jnp.where(lane == part * tiles + tile, place, places)
    wide = jnp.concatenate([places, places], axis=0).astype(jnp.float32).T
    index_ref[...] = wide[: 2 * tiles].astype(jnp.int32)
    copy = pltpu.make_async_copy(index_ref, place_ref, sem)
    copy.start()
    copy.wait()
    copy_pieces(place_ref, x_ref, out_ref, tiles)


def pick_second(spread, tiles):
    owners = spread.shape[0]
    return pl.pallas_call(
        pick_second_kernel,
        in_specs=[pl.BlockSpec(memory_space=pltpu.VMEM)],
        out_specs=[pl.BlockSpec(memory_space=pltpu.VMEM)] * 2,
        out_shape=[
            jax.ShapeDtypeStruct((owners, tiles, GROUP, LANES), jnp.bfloat16),
            jax.ShapeDtypeStruct((2 * tiles, LANES), jnp.int32),
        ],
        scratch_shapes=[
            pltpu.VMEM((owners * GROUP, LANES), jnp.float32),
            pltpu.SMEM((2 * tiles, LANES), jnp.int32),
            pltpu.SemaphoreType.DMA,
        ],
        compiler_params=pltpu.CompilerParams(vmem_limit_bytes=24 * 2**20),
        name="pick_second",
    )(spread)


def pick_first(index, spread, tiles):
    owners = spread.shape[0]
    return pl.pallas_call(
        lambda place_ref, x_ref, out_ref: copy_pieces(place_ref, x_ref, out_ref, 0),
        in_specs=[
            pl.BlockSpec(memory_space=pltpu.SMEM),
            pl.BlockSpec(memory_space=pltpu.VMEM),
        ],
        out_specs=pl.BlockSpec(memory_space=pltpu.VMEM),
        out_shape=jax.ShapeDtypeStruct((owners, tiles, GROUP, LANES), jnp.bfloat16),
        compiler_params=pltpu.CompilerParams(vmem_limit_bytes=24 * 2**20),
        name="pick_first",
    )(index, spread)


def correlate_kernel(scaling, win_ref, a_ref, *refs):
    windows = a_ref.shape[2]
    b_refs, table_hbm = refs[:windows], refs[windows]
    out_hbm, stack_ref, table_ref, panel_ref, sem, out_sems = refs[windows + 1 :]
    tiles = last = a_ref.shape[3]
    _, lane_groups, groups = b_refs[0].shape[:3]
    bins = lane_groups * LANES
    channels = groups * GROUP
    places = [
        [lax.rem(group + distance + groups - win_ref[0], groups) for group in range(groups)]
        for distance in range(windows)
    ]
    table_copy = pltpu.make_async_copy(table_hbm, table_ref, sem)

    def out_copy(tile):
        slot = lax.rem(tile, 2)
        return pltpu.make_async_copy(panel_ref.at[slot], out_hbm.at[:, tile], out_sems.at[slot])

    def cross(step, lane_group, slot):
        lanes = lane_group * LANES
        a = [
            [a_ref[part, lane_group, w, step].astype(jnp.float32) for part in range(2)]
            for w in range(windows)
        ]
        for pair in range(groups // 2):
            b = [
                [
                    [
                        b_refs[w][part, lane_group, places[w][pair * 2 + half], step].astype(
                            jnp.float32
                        )
                        for part in range(2)
                    ]
                    for w in range(windows)
                ]
                for half in range(2)
            ]
            for i in range(GROUP):
                rows = [[None, None], [None, None]]
                for w in range(windows):
                    a0 = jnp.broadcast_to(a[w][0][i : i + 1], (GROUP, LANES))
                    a1 = jnp.broadcast_to(a[w][1][i : i + 1], (GROUP, LANES))
                    for half in range(2):
                        b0, b1 = b[half][w]
                        real = a0 * b0 + a1 * b1
                        imag = a1 * b0 - a0 * b1
                        if w:
                            real += rows[half][0]
                            imag += rows[half][1]
                        rows[half] = [real, imag]
                start = i * channels + pair * 2 * GROUP
                for part in range(2):
                    joined = jnp.concatenate([rows[0][part], rows[1][part]], axis=0)
                    stack_ref[
                        slot, start : start + 2 * GROUP, pl.ds(part * bins + lanes, LANES)
                    ] = joined.astype(jnp.bfloat16)

    def lagged(chunk, slot):
        columns = pl.ds(chunk * 2 * LANES, 2 * LANES)
        rows = jnp.dot(stack_ref[slot], table_ref[:, columns], preferred_element_type=jnp.float32)
        rows = (rows * scaling).astype(jnp.bfloat16)
        panel_ref[slot, :, :, columns] = rows.reshape(GROUP, channels, 2 * LANES)

    def run(step, with_cross, with_lagged):
        for chunk in range(lane_groups // 2):
            if with_lagged:
                lagged(chunk, lax.rem(step + 1, 2))
            if with_cross:
                cross(step, chunk * 2, lax.rem(step, 2))
                cross(step, chunk * 2 + 1, lax.rem(step, 2))

    def one_step(step, carry):
        @pl.when(step > 2)
        def _():
            out_copy(step - 3).wait()

        @pl.when(step == 0)
        def _():
            table_copy.start()
            run(step, True, False)
            table_copy.wait()

        @pl.when(jnp.logical_and(step > 0, step < last))
        def _():
            run(step, True, True)

        @pl.when(step == last)
        def _():
            run(step, False, True)

        @pl.when(step > 0)
        def _():
            out_copy(step - 1).start()

        return carry

    lax.fori_loop(0, tiles + 1, one_step, 0)
    for tile in range(max(tiles - 2, 0), tiles):
        out_copy(tile).wait()


def correlate(win, a, b, table):
    _, lane_groups, windows, tiles = a.shape[:4]
    channels = b[0].shape[2] * GROUP
    bins = lane_groups * LANES
    lags = table.shape[1]
    scaling = 1.0 / math.sqrt(windows * bins)
    return pl.pallas_call(
        functools.partial(correlate_kernel, scaling),
        in_specs=[pl.BlockSpec(memory_space=pltpu.SMEM)]
        + [pl.BlockSpec(memory_space=pltpu.VMEM)] * (1 + len(b))
        + [pl.BlockSpec(memory_space=pltpu.HBM)],
        out_specs=pl.BlockSpec(memory_space=pltpu.HBM),
        out_shape=jax.ShapeDtypeStruct((GROUP, tiles, channels, lags), jnp.bfloat16),
        scratch_shapes=[
            pltpu.VMEM((2, GROUP * channels, 2 * bins), jnp.bfloat16),
            pltpu.VMEM(table.shape, table.dtype),
            pltpu.VMEM((2, GROUP, channels, lags), jnp.bfloat16),
            pltpu.SemaphoreType.DMA,
            pltpu.SemaphoreType.DMA((2,)),
        ],
        compiler_params=pltpu.CompilerParams(vmem_limit_bytes=48 * 2**20),
        name="correlate",
    )(win, a, *b, table)


def settle_kernel(win_ref, *refs):
    refs[-1][0] = win_ref[0]


def settle(win, arrays):
    return pl.pallas_call(
        settle_kernel,
        in_specs=[pl.BlockSpec(memory_space=pltpu.SMEM)]
        + [pl.BlockSpec(memory_space=pl.ANY)] * len(arrays),
        out_specs=pl.BlockSpec(memory_space=pltpu.SMEM),
        out_shape=jax.ShapeDtypeStruct(win.shape, win.dtype),
        compiler_params=pltpu.CompilerParams(vmem_limit_bytes=2**20),
        cost_estimate=pl.CostEstimate(flops=SETTLE_FLOPS, bytes_accessed=0, transcendentals=0),
        name="settle",
    )(win, *arrays)


def lag_rows_table(bin_total):
    bin_index = jnp.arange(bin_total, dtype=jnp.int32) + F0
    lag_index = jnp.arange(LAGS, dtype=jnp.int32) - LAGS // 2
    wrapped = bin_index[:, None] * lag_index[None, :] % NS
    phases = wrapped.astype(jnp.float32) * (2.0 * math.pi / NS)
    return jnp.concatenate([jnp.cos(phases), -jnp.sin(phases)], axis=0).astype(jnp.bfloat16)


def local(spectra, send_blocks, tile_slots):
    windows, owners = lax.axis_size("win"), lax.axis_size("pair")
    blocks, _, parts, channels, bins = spectra.shape
    tiles = tile_slots.shape[0]
    groups = channels // GROUP
    exchange = lambda x: lax.all_to_all(x, "pair", split_axis=0, concat_axis=0, tiled=True)
    pieces = (parts, bins // LANES, groups, tiles, GROUP, LANES)

    win = lax.axis_index("win").astype(jnp.int32).reshape(1)
    outgoing = whiten_spread(win, spectra, send_blocks[0].T, tile_slots.T)
    spread = exchange(outgoing.reshape(owners, blocks + 1, GROUP, LANES))
    spread, table = lax.optimization_barrier((spread, lag_rows_table(bins)))
    second, index = pick_second(spread, tiles)
    first = pick_first(index, spread, tiles)
    turn = [
        (w * owners + j, (w + j) % windows * owners + j)
        for w in range(windows)
        for j in range(owners)
    ]
    first = lax.ppermute(first, ("win", "pair"), turn)
    second = exchange(second)
    second, first = lax.optimization_barrier((second, first))
    b = [second]
    for distance in range(1, windows):
        step = [(w, (w + distance) % windows) for w in range(windows)]
        b.append(lax.ppermute(second, "win", step))
    win = settle(win, b[windows // 2 : windows // 2 + 1])
    a = exchange(first).reshape(pieces)
    return correlate(win, a, [x.reshape(pieces) for x in b], table)


def solution(mesh):
    in_specs = (P("pair", "win", None, None, None), P("pair", None, None), P("pair", None))
    out_specs = P("win", "pair", None, None)
    return jax.shard_map(local, mesh=mesh, in_specs=in_specs, out_specs=out_specs, check_vma=False)
```

```python
import functools
import math

import jax
import jax.numpy as jnp
from jax import lax
from jax.experimental import pallas as pl
from jax.experimental.pallas import tpu as pltpu
from jax.sharding import PartitionSpec as P

LAGS = 1024
NS = 4096
F0 = 64
BAND = 64
LANES = 128
GROUP = 8
HALF = 64
SETTLE_FLOPS = 8 * 10**9


def whiten_kernel(win_ref, x_ref, sent_ref, slots_ref, out_ref, table_ref):
    blocks, _, _, channels, _ = x_ref.shape
    _, lane_groups, groups = out_ref.shape[:3]
    row_band = lax.broadcasted_iota(jnp.int32, (LANES, LANES), 0) // BAND
    column_band = lax.broadcasted_iota(jnp.int32, (LANES, LANES), 1) // BAND
    ones = jnp.where(row_band == column_band, 1.0, 0.0).astype(jnp.bfloat16)
    ones = jnp.concatenate([ones, ones, ones], axis=0)
    places = [lax.rem(group + groups - win_ref[0], groups) for group in range(groups)]
    for lane_group in range(lane_groups):
        lanes = slice(lane_group * LANES, (lane_group + 1) * LANES)
        real, imag = [
            x_ref[:, 0, part, :, lanes].astype(jnp.float32).reshape(blocks * channels, LANES)
            for part in range(2)
        ]
        rest = real * real + imag * imag
        terms = []
        for _ in range(3):
            terms.append(rest.astype(jnp.bfloat16))
            rest = rest - terms[-1].astype(jnp.float32)
        power = jnp.dot(jnp.concatenate(terms, axis=1), ones, preferred_element_type=jnp.float32)
        scale = lax.rsqrt(power * (1.0 / (2 * BAND)) + 1e-06)
        for part, rows in enumerate((real * scale, imag * scale)):
            rows = rows.reshape(blocks, groups, GROUP, LANES)
            for group in range(groups):
                out_ref[part, lane_group, places[group], :blocks] = rows[:, group].astype(
                    jnp.bfloat16
                )

    @pl.when(pl.program_id(0) == 0)
    def _():
        table_ref[...] = jnp.zeros_like(table_ref)
        table_ref[0:2, : sent_ref.shape[1]] = sent_ref[...].astype(jnp.float32)
        table_ref[2:4, : slots_ref.shape[1]] = slots_ref[...].astype(jnp.float32)

    piece = table_ref[...].astype(jnp.bfloat16)
    shape = out_ref.shape
    out_ref[:, :, :, blocks] = jnp.broadcast_to(piece, shape[:3] + shape[4:])


def whiten_spread(win, spectra, sent, slots):
    blocks, _, parts, channels, bins = spectra.shape
    shape = (parts, bins // LANES, channels // GROUP, blocks + 1, GROUP, LANES)
    steps = 2
    width = bins // steps
    return pl.pallas_call(
        whiten_kernel,
        grid=(steps,),
        in_specs=[
            pl.BlockSpec(memory_space=pltpu.SMEM),
            pl.BlockSpec((blocks, 1, parts, channels, width), lambda g: (0, 0, 0, 0, g)),
            pl.BlockSpec(sent.shape, lambda g: (0, 0)),
            pl.BlockSpec(slots.shape, lambda g: (0, 0)),
        ],
        out_specs=pl.BlockSpec(
            (parts, width // LANES) + shape[2:], lambda g: (0, g, 0, 0, 0, 0)
        ),
        out_shape=jax.ShapeDtypeStruct(shape, jnp.bfloat16),
        scratch_shapes=[pltpu.VMEM((GROUP, LANES), jnp.float32)],
        compiler_params=pltpu.CompilerParams(vmem_limit_bytes=60 * 2**20),
        name="whiten_spread",
    )(win, spectra, sent, slots)


def copy_pieces(place_ref, x_ref, out_ref, start):
    flat = x_ref.reshape((x_ref.shape[0] * x_ref.shape[1],) + x_ref.shape[2:])

    def one_owner(owner, carry):
        for tile in range(out_ref.shape[1]):
            out_ref[owner, tile] = flat[place_ref[start + tile, owner]]
        return carry

    lax.fori_loop(0, out_ref.shape[0], one_owner, 0, unroll=4)


def pick_second_kernel(x_ref, out_ref, index_ref, table_ref, place_ref, sem):
    owners, stride = x_ref.shape[:2]
    tiles = out_ref.shape[1]
    table_ref[...] = x_ref[:, stride - 1].astype(jnp.float32).reshape(table_ref.shape)
    sent = [table_ref[pl.ds(k, owners, stride=GROUP), :] for k in range(2)]
    lane = lax.broadcasted_iota(jnp.int32, (owners, LANES), 1)
    by_owner = jnp.concatenate(sent, axis=0).T[:owners].astype(jnp.int32)
    by_owner = by_owner + stride * (lane % HALF)
    places = jnp.zeros((owners, LANES), jnp.int32)
    for part in range(2):
        slots = table_ref[pl.ds(2 + part, owners, stride=GROUP), :].astype(jnp.int32)
        for tile in range(tiles):
            slot = slots[:, tile : tile + 1]
            hit = lane == (slot % 2) * HALF + slot // 2
            place = jnp.sum(jnp.where(hit, by_owner, 0), axis=1, keepdims=True)
            places = jnp.where(lane == part * tiles + tile, place, places)
    wide = jnp.concatenate([places, places], axis=0).astype(jnp.float32).T
    index_ref[...] = wide[: 2 * tiles].astype(jnp.int32)
    copy = pltpu.make_async_copy(index_ref, place_ref, sem)
    copy.start()
    copy.wait()
    copy_pieces(place_ref, x_ref, out_ref, tiles)


def pick_second(spread, tiles):
    owners = spread.shape[0]
    return pl.pallas_call(
        pick_second_kernel,
        in_specs=[pl.BlockSpec(memory_space=pltpu.VMEM)],
        out_specs=[pl.BlockSpec(memory_space=pltpu.VMEM)] * 2,
        out_shape=[
            jax.ShapeDtypeStruct((owners, tiles, GROUP, LANES), jnp.bfloat16),
            jax.ShapeDtypeStruct((2 * tiles, LANES), jnp.int32),
        ],
        scratch_shapes=[
            pltpu.VMEM((owners * GROUP, LANES), jnp.float32),
            pltpu.SMEM((2 * tiles, LANES), jnp.int32),
            pltpu.SemaphoreType.DMA,
        ],
        compiler_params=pltpu.CompilerParams(vmem_limit_bytes=24 * 2**20),
        name="pick_second",
    )(spread)


def pick_first(index, spread, tiles):
    owners = spread.shape[0]
    return pl.pallas_call(
        lambda place_ref, x_ref, out_ref: copy_pieces(place_ref, x_ref, out_ref, 0),
        in_specs=[
            pl.BlockSpec(memory_space=pltpu.SMEM),
            pl.BlockSpec(memory_space=pltpu.VMEM),
        ],
        out_specs=pl.BlockSpec(memory_space=pltpu.VMEM),
        out_shape=jax.ShapeDtypeStruct((owners, tiles, GROUP, LANES), jnp.bfloat16),
        compiler_params=pltpu.CompilerParams(vmem_limit_bytes=24 * 2**20),
        name="pick_first",
    )(index, spread)


def correlate_kernel(scaling, win_ref, a_ref, *refs):
    windows = a_ref.shape[2]
    b_refs, table_hbm = refs[:windows], refs[windows]
    out_ref, stack_ref, table_ref, sem = refs[windows + 1 :]
    step = pl.program_id(0)
    last = pl.num_programs(0) - 1
    _, lane_groups, groups = b_refs[0].shape[:3]
    bins = lane_groups * LANES
    channels = groups * GROUP
    places = [
        [lax.rem(group + distance + groups - win_ref[0], groups) for group in range(groups)]
        for distance in range(windows)
    ]
    table_copy = pltpu.make_async_copy(table_hbm, table_ref, sem)

    def cross(lane_group, slot):
        lanes = lane_group * LANES
        a = [
            [a_ref[part, lane_group, w, step].astype(jnp.float32) for part in range(2)]
            for w in range(windows)
        ]
        for pair in range(groups // 2):
            b = [
                [
                    [
                        b_refs[w][part, lane_group, places[w][pair * 2 + half], step].astype(
                            jnp.float32
                        )
                        for part in range(2)
                    ]
                    for w in range(windows)
                ]
                for half in range(2)
            ]
            for i in range(GROUP):
                rows = [[None, None], [None, None]]
                for w in range(windows):
                    a0 = jnp.broadcast_to(a[w][0][i : i + 1], (GROUP, LANES))
                    a1 = jnp.broadcast_to(a[w][1][i : i + 1], (GROUP, LANES))
                    for half in range(2):
                        b0, b1 = b[half][w]
                        real = a0 * b0 + a1 * b1
                        imag = a1 * b0 - a0 * b1
                        if w:
                            real += rows[half][0]
                            imag += rows[half][1]
                        rows[half] = [real, imag]
                start = i * channels + pair * 2 * GROUP
                for part in range(2):
                    joined = jnp.concatenate([rows[0][part], rows[1][part]], axis=0)
                    stack_ref[
                        slot, start : start + 2 * GROUP, pl.ds(part * bins + lanes, LANES)
                    ] = joined.astype(jnp.bfloat16)

    def lagged(chunk, slot):
        columns = pl.ds(chunk * 2 * LANES, 2 * LANES)
        rows = jnp.dot(stack_ref[slot], table_ref[:, columns], preferred_element_type=jnp.float32)
        rows = (rows * scaling).astype(jnp.bfloat16)
        out_ref[:, 0, :, columns] = rows.reshape(GROUP, channels, 2 * LANES)

    def run(with_cross, with_lagged):
        for chunk in range(lane_groups // 2):
            if with_lagged:
                lagged(chunk, lax.rem(step + 1, 2))
            if with_cross:
                cross(chunk * 2, lax.rem(step, 2))
                cross(chunk * 2 + 1, lax.rem(step, 2))

    @pl.when(step == 0)
    def _():
        table_copy.start()
        run(True, False)
        table_copy.wait()

    @pl.when(jnp.logical_and(step > 0, step < last))
    def _():
        run(True, True)

    @pl.when(step == last)
    def _():
        run(False, True)


def correlate(win, a, b, table):
    _, lane_groups, windows, tiles = a.shape[:4]
    channels = b[0].shape[2] * GROUP
    bins = lane_groups * LANES
    lags = table.shape[1]
    scaling = 1.0 / math.sqrt(windows * bins)
    whole = lambda x: pl.BlockSpec(x.shape, lambda t: (0,) * len(x.shape))
    return pl.pallas_call(
        functools.partial(correlate_kernel, scaling),
        grid=(tiles + 1,),
        in_specs=[pl.BlockSpec(memory_space=pltpu.SMEM)]
        + [whole(x) for x in (a, *b)]
        + [pl.BlockSpec(memory_space=pltpu.HBM)],
        out_specs=pl.BlockSpec(
            (GROUP, 1, channels, lags), lambda t: (0, jnp.maximum(t - 1, 0), 0, 0)
        ),
        out_shape=jax.ShapeDtypeStruct((GROUP, tiles, channels, lags), jnp.bfloat16),
        scratch_shapes=[
            pltpu.VMEM((2, GROUP * channels, 2 * bins), jnp.bfloat16),
            pltpu.VMEM(table.shape, table.dtype),
            pltpu.SemaphoreType.DMA,
        ],
        compiler_params=pltpu.CompilerParams(vmem_limit_bytes=48 * 2**20),
        name="correlate",
    )(win, a, *b, table)


def settle_kernel(win_ref, *refs):
    refs[-1][0] = win_ref[0]


def settle(win, arrays):
    return pl.pallas_call(
        settle_kernel,
        in_specs=[pl.BlockSpec(memory_space=pltpu.SMEM)]
        + [pl.BlockSpec(memory_space=pl.ANY)] * len(arrays),
        out_specs=pl.BlockSpec(memory_space=pltpu.SMEM),
        out_shape=jax.ShapeDtypeStruct(win.shape, win.dtype),
        compiler_params=pltpu.CompilerParams(vmem_limit_bytes=2**20),
        cost_estimate=pl.CostEstimate(flops=SETTLE_FLOPS, bytes_accessed=0, transcendentals=0),
        name="settle",
    )(win, *arrays)


def lag_rows_table(bin_total):
    fine = 16
    lag_index = jnp.arange(LAGS, dtype=jnp.int32) - LAGS // 2

    def turns(bins):
        wrapped = bins[:, None] * lag_index[None, :] % NS
        phases = wrapped.astype(jnp.float32) * (2.0 * math.pi / NS)
        return jnp.cos(phases), jnp.sin(phases)

    coarse_bins = jnp.arange(bin_total // fine, dtype=jnp.int32) * fine + F0
    pairs = turns(jnp.concatenate([coarse_bins, jnp.arange(fine, dtype=jnp.int32)]))
    cosine, sine = lax.optimization_barrier(pairs)
    coarse = [x[:-fine, None, :] for x in (cosine, sine)]
    small = [x[None, -fine:, :] for x in (cosine, sine)]
    real = coarse[0] * small[0] - coarse[1] * small[1]
    imag = coarse[1] * small[0] + coarse[0] * small[1]
    table = jnp.stack([real, -imag]).astype(jnp.bfloat16)
    return table.reshape(2 * bin_total, LAGS)


def local(spectra, send_blocks, tile_slots):
    windows, owners = lax.axis_size("win"), lax.axis_size("pair")
    blocks, _, parts, channels, bins = spectra.shape
    tiles = tile_slots.shape[0]
    groups = channels // GROUP
    exchange = lambda x: lax.all_to_all(x, "pair", split_axis=0, concat_axis=0, tiled=True)
    pieces = (parts, bins // LANES, groups, tiles, GROUP, LANES)

    win = lax.axis_index("win").astype(jnp.int32).reshape(1)
    outgoing = whiten_spread(win, spectra, send_blocks[0].T, tile_slots.T)
    spread = exchange(outgoing.reshape(owners, blocks + 1, GROUP, LANES))
    spread, table = lax.optimization_barrier((spread, lag_rows_table(bins)))
    second, index = pick_second(spread, tiles)
    first = pick_first(index, spread, tiles)
    turn = [
        (w * owners + j, (w + j) % windows * owners + j)
        for w in range(windows)
        for j in range(owners)
    ]
    first = lax.ppermute(first, ("win", "pair"), turn)
    second = exchange(second)
    second, first = lax.optimization_barrier((second, first))
    b = [second]
    for distance in range(1, windows):
        step = [(w, (w + distance) % windows) for w in range(windows)]
        b.append(lax.ppermute(second, "win", step))
    win = settle(win, b[windows // 2 : windows // 2 + 1])
    a = exchange(first).reshape(pieces)
    return correlate(win, a, [x.reshape(pieces) for x in b], table)


def solution(mesh):
    in_specs = (P("pair", "win", None, None, None), P("pair", None, None), P("pair", None))
    out_specs = P("win", "pair", None, None)
    return jax.shard_map(local, mesh=mesh, in_specs=in_specs, out_specs=out_specs, check_vma=False)
```

```python
import functools
import math

import jax
import jax.numpy as jnp
from jax import lax
from jax.experimental import pallas as pl
from jax.experimental.pallas import tpu as pltpu
from jax.sharding import PartitionSpec as P

LAGS = 1024
NS = 4096
F0 = 64
BAND = 64
LANES = 128
GROUP = 8
HALF = 64
SETTLE_FLOPS = 8 * 10**9


def whiten_kernel(win_ref, x_ref, sent_ref, slots_ref, out_ref, table_ref):
    blocks, _, _, channels, _ = x_ref.shape
    _, lane_groups, groups = out_ref.shape[:3]
    row_band = lax.broadcasted_iota(jnp.int32, (LANES, LANES), 0) // BAND
    column_band = lax.broadcasted_iota(jnp.int32, (LANES, LANES), 1) // BAND
    ones = jnp.where(row_band == column_band, 1.0, 0.0).astype(jnp.bfloat16)
    ones = jnp.concatenate([ones, ones, ones], axis=0)
    places = [lax.rem(group + groups - win_ref[0], groups) for group in range(groups)]
    for lane_group in range(lane_groups):
        lanes = slice(lane_group * LANES, (lane_group + 1) * LANES)
        real, imag = [
            x_ref[:, 0, part, :, lanes].astype(jnp.float32).reshape(blocks * channels, LANES)
            for part in range(2)
        ]
        rest = real * real + imag * imag
        terms = []
        for _ in range(3):
            terms.append(rest.astype(jnp.bfloat16))
            rest = rest - terms[-1].astype(jnp.float32)
        power = jnp.dot(jnp.concatenate(terms, axis=1), ones, preferred_element_type=jnp.float32)
        scale = lax.rsqrt(power * (1.0 / (2 * BAND)) + 1e-06)
        for part, rows in enumerate((real * scale, imag * scale)):
            rows = rows.reshape(blocks, groups, GROUP, LANES)
            for group in range(groups):
                out_ref[part, lane_group, places[group], :blocks] = rows[:, group].astype(
                    jnp.bfloat16
                )

    @pl.when(pl.program_id(0) == 0)
    def _():
        table_ref[...] = jnp.zeros_like(table_ref)
        table_ref[0:2, : sent_ref.shape[1]] = sent_ref[...].astype(jnp.float32)
        table_ref[2:4, : slots_ref.shape[1]] = slots_ref[...].astype(jnp.float32)

    piece = table_ref[...].astype(jnp.bfloat16)
    shape = out_ref.shape
    out_ref[:, :, :, blocks] = jnp.broadcast_to(piece, shape[:3] + shape[4:])


def whiten_spread(win, spectra, sent, slots):
    blocks, _, parts, channels, bins = spectra.shape
    shape = (parts, bins // LANES, channels // GROUP, blocks + 1, GROUP, LANES)
    steps = 1
    width = bins // steps
    return pl.pallas_call(
        whiten_kernel,
        grid=(steps,),
        in_specs=[
            pl.BlockSpec(memory_space=pltpu.SMEM),
            pl.BlockSpec((blocks, 1, parts, channels, width), lambda g: (0, 0, 0, 0, g)),
            pl.BlockSpec(sent.shape, lambda g: (0, 0)),
            pl.BlockSpec(slots.shape, lambda g: (0, 0)),
        ],
        out_specs=pl.BlockSpec(
            (parts, width // LANES) + shape[2:], lambda g: (0, g, 0, 0, 0, 0)
        ),
        out_shape=jax.ShapeDtypeStruct(shape, jnp.bfloat16),
        scratch_shapes=[pltpu.VMEM((GROUP, LANES), jnp.float32)],
        compiler_params=pltpu.CompilerParams(vmem_limit_bytes=60 * 2**20),
        name="whiten_spread",
    )(win, spectra, sent, slots)


def copy_pieces(place_ref, x_ref, out_ref, start):
    flat = x_ref.reshape((x_ref.shape[0] * x_ref.shape[1],) + x_ref.shape[2:])

    def one_owner(owner, carry):
        for tile in range(out_ref.shape[1]):
            out_ref[owner, tile] = flat[place_ref[start + tile, owner]]
        return carry

    lax.fori_loop(0, out_ref.shape[0], one_owner, 0, unroll=4)


def pick_second_kernel(x_ref, out_ref, index_ref, table_ref, place_ref, sem):
    owners, stride = x_ref.shape[:2]
    tiles = out_ref.shape[1]
    table_ref[...] = x_ref[:, stride - 1].astype(jnp.float32).reshape(table_ref.shape)
    sent = [table_ref[pl.ds(k, owners, stride=GROUP), :] for k in range(2)]
    lane = lax.broadcasted_iota(jnp.int32, (owners, LANES), 1)
    by_owner = jnp.concatenate(sent, axis=0).T[:owners].astype(jnp.int32)
    by_owner = by_owner + stride * (lane % HALF)
    places = jnp.zeros((owners, LANES), jnp.int32)
    for part in range(2):
        slots = table_ref[pl.ds(2 + part, owners, stride=GROUP), :].astype(jnp.int32)
        for tile in range(tiles):
            slot = slots[:, tile : tile + 1]
            hit = lane == (slot % 2) * HALF + slot // 2
            place = jnp.sum(jnp.where(hit, by_owner, 0), axis=1, keepdims=True)
            places = jnp.where(lane == part * tiles + tile, place, places)
    wide = jnp.concatenate([places, places], axis=0).astype(jnp.float32).T
    index_ref[...] = wide[: 2 * tiles].astype(jnp.int32)
    copy = pltpu.make_async_copy(index_ref, place_ref, sem)
    copy.start()
    copy.wait()
    copy_pieces(place_ref, x_ref, out_ref, tiles)


def pick_second(spread, tiles):
    owners = spread.shape[0]
    return pl.pallas_call(
        pick_second_kernel,
        in_specs=[pl.BlockSpec(memory_space=pltpu.VMEM)],
        out_specs=[pl.BlockSpec(memory_space=pltpu.VMEM)] * 2,
        out_shape=[
            jax.ShapeDtypeStruct((owners, tiles, GROUP, LANES), jnp.bfloat16),
            jax.ShapeDtypeStruct((2 * tiles, LANES), jnp.int32),
        ],
        scratch_shapes=[
            pltpu.VMEM((owners * GROUP, LANES), jnp.float32),
            pltpu.SMEM((2 * tiles, LANES), jnp.int32),
            pltpu.SemaphoreType.DMA,
        ],
        compiler_params=pltpu.CompilerParams(vmem_limit_bytes=24 * 2**20),
        name="pick_second",
    )(spread)


def pick_first(index, spread, tiles):
    owners = spread.shape[0]
    return pl.pallas_call(
        lambda place_ref, x_ref, out_ref: copy_pieces(place_ref, x_ref, out_ref, 0),
        in_specs=[
            pl.BlockSpec(memory_space=pltpu.SMEM),
            pl.BlockSpec(memory_space=pltpu.VMEM),
        ],
        out_specs=pl.BlockSpec(memory_space=pltpu.VMEM),
        out_shape=jax.ShapeDtypeStruct((owners, tiles, GROUP, LANES), jnp.bfloat16),
        compiler_params=pltpu.CompilerParams(vmem_limit_bytes=24 * 2**20),
        name="pick_first",
    )(index, spread)


def correlate_kernel(scaling, win_ref, a_ref, *refs):
    windows = a_ref.shape[2]
    b_refs, table_hbm = refs[:windows], refs[windows]
    out_ref, stack_ref, table_ref, sem = refs[windows + 1 :]
    step = pl.program_id(0)
    last = pl.num_programs(0) - 1
    _, lane_groups, groups = b_refs[0].shape[:3]
    bins = lane_groups * LANES
    channels = groups * GROUP
    places = [
        [lax.rem(group + distance + groups - win_ref[0], groups) for group in range(groups)]
        for distance in range(windows)
    ]
    table_copy = pltpu.make_async_copy(table_hbm, table_ref, sem)

    def cross(lane_group, slot):
        lanes = lane_group * LANES
        a = [
            [a_ref[part, lane_group, w, step].astype(jnp.float32) for part in range(2)]
            for w in range(windows)
        ]
        for pair in range(groups // 2):
            b = [
                [
                    [
                        b_refs[w][part, lane_group, places[w][pair * 2 + half], step].astype(
                            jnp.float32
                        )
                        for part in range(2)
                    ]
                    for w in range(windows)
                ]
                for half in range(2)
            ]
            for i in range(GROUP):
                rows = [[None, None], [None, None]]
                for w in range(windows):
                    a0 = jnp.broadcast_to(a[w][0][i : i + 1], (GROUP, LANES))
                    a1 = jnp.broadcast_to(a[w][1][i : i + 1], (GROUP, LANES))
                    for half in range(2):
                        b0, b1 = b[half][w]
                        real = a0 * b0 + a1 * b1
                        imag = a1 * b0 - a0 * b1
                        if w:
                            real += rows[half][0]
                            imag += rows[half][1]
                        rows[half] = [real, imag]
                start = i * channels + pair * 2 * GROUP
                for part in range(2):
                    joined = jnp.concatenate([rows[0][part], rows[1][part]], axis=0)
                    stack_ref[
                        slot, start : start + 2 * GROUP, pl.ds(part * bins + lanes, LANES)
                    ] = joined.astype(jnp.bfloat16)

    def lagged(chunk, slot):
        columns = pl.ds(chunk * 2 * LANES, 2 * LANES)
        rows = jnp.dot(stack_ref[slot], table_ref[:, columns], preferred_element_type=jnp.float32)
        rows = (rows * scaling).astype(jnp.bfloat16)
        out_ref[:, 0, :, columns] = rows.reshape(GROUP, channels, 2 * LANES)

    def run(with_cross, with_lagged):
        for chunk in range(lane_groups // 2):
            if with_lagged:
                lagged(chunk, lax.rem(step + 1, 2))
            if with_cross:
                cross(chunk * 2, lax.rem(step, 2))
                cross(chunk * 2 + 1, lax.rem(step, 2))

    @pl.when(step == 0)
    def _():
        table_copy.start()
        run(True, False)
        table_copy.wait()

    @pl.when(jnp.logical_and(step > 0, step < last))
    def _():
        run(True, True)

    @pl.when(step == last)
    def _():
        run(False, True)


def correlate(win, a, b, table):
    _, lane_groups, windows, tiles = a.shape[:4]
    channels = b[0].shape[2] * GROUP
    bins = lane_groups * LANES
    lags = table.shape[1]
    scaling = 1.0 / math.sqrt(windows * bins)
    whole = lambda x: pl.BlockSpec(x.shape, lambda t: (0,) * len(x.shape))
    return pl.pallas_call(
        functools.partial(correlate_kernel, scaling),
        grid=(tiles + 1,),
        in_specs=[pl.BlockSpec(memory_space=pltpu.SMEM)]
        + [whole(x) for x in (a, *b)]
        + [pl.BlockSpec(memory_space=pltpu.HBM)],
        out_specs=pl.BlockSpec(
            (GROUP, 1, channels, lags), lambda t: (0, jnp.maximum(t - 1, 0), 0, 0)
        ),
        out_shape=jax.ShapeDtypeStruct((GROUP, tiles, channels, lags), jnp.bfloat16),
        scratch_shapes=[
            pltpu.VMEM((2, GROUP * channels, 2 * bins), jnp.bfloat16),
            pltpu.VMEM(table.shape, table.dtype),
            pltpu.SemaphoreType.DMA,
        ],
        compiler_params=pltpu.CompilerParams(vmem_limit_bytes=48 * 2**20),
        name="correlate",
    )(win, a, *b, table)


def settle_kernel(win_ref, *refs):
    refs[-1][0] = win_ref[0]


def settle(win, arrays):
    return pl.pallas_call(
        settle_kernel,
        in_specs=[pl.BlockSpec(memory_space=pltpu.SMEM)]
        + [pl.BlockSpec(memory_space=pl.ANY)] * len(arrays),
        out_specs=pl.BlockSpec(memory_space=pltpu.SMEM),
        out_shape=jax.ShapeDtypeStruct(win.shape, win.dtype),
        compiler_params=pltpu.CompilerParams(vmem_limit_bytes=2**20),
        cost_estimate=pl.CostEstimate(flops=SETTLE_FLOPS, bytes_accessed=0, transcendentals=0),
        name="settle",
    )(win, *arrays)


def lag_rows_table(bin_total):
    bin_index = jnp.arange(bin_total, dtype=jnp.int32) + F0
    lag_index = jnp.arange(LAGS, dtype=jnp.int32) - LAGS // 2
    wrapped = bin_index[:, None] * lag_index[None, :] % NS
    phases = wrapped.astype(jnp.float32) * (2.0 * math.pi / NS)
    return jnp.concatenate([jnp.cos(phases), -jnp.sin(phases)], axis=0).astype(jnp.bfloat16)


def local(spectra, send_blocks, tile_slots):
    windows, owners = lax.axis_size("win"), lax.axis_size("pair")
    blocks, _, parts, channels, bins = spectra.shape
    tiles = tile_slots.shape[0]
    groups = channels // GROUP
    exchange = lambda x: lax.all_to_all(x, "pair", split_axis=0, concat_axis=0, tiled=True)
    pieces = (parts, bins // LANES, groups, tiles, GROUP, LANES)

    win = lax.axis_index("win").astype(jnp.int32).reshape(1)
    outgoing = whiten_spread(win, spectra, send_blocks[0].T, tile_slots.T)
    spread = exchange(outgoing.reshape(owners, blocks + 1, GROUP, LANES))
    spread, table = lax.optimization_barrier((spread, lag_rows_table(bins)))
    second, index = pick_second(spread, tiles)
    first = pick_first(index, spread, tiles)
    turn = [
        (w * owners + j, (w + j) % windows * owners + j)
        for w in range(windows)
        for j in range(owners)
    ]
    first = lax.ppermute(first, ("win", "pair"), turn)
    second = exchange(second)
    second, first = lax.optimization_barrier((second, first))
    b = [second]
    for distance in range(1, windows):
        step = [(w, (w + distance) % windows) for w in range(windows)]
        b.append(lax.ppermute(second, "win", step))
    win = settle(win, b[windows // 2 : windows // 2 + 1])
    a = exchange(first).reshape(pieces)
    return correlate(win, a, [x.reshape(pieces) for x in b], table)


def solution(mesh):
    in_specs = (P("pair", "win", None, None, None), P("pair", None, None), P("pair", None))
    out_specs = P("win", "pair", None, None)
    return jax.shard_map(local, mesh=mesh, in_specs=in_specs, out_specs=out_specs, check_vma=False)
```
